512 devices in a mesh: ctx: 64 (over z, x, y_hi), tp: 8 (over y_lo, core).
Axes of the slice: x: 4, y: 8 (y_hi: 2, y_lo: 4; y = y_hi * 4 + y_lo), z: 8, core: 2. Of those that a mesh axis runs over, the one named last changes fastest.
Arguments:
- queries: bfloat16 [16384, 4096], P('ctx', 'tp'), may hold values from -6 to 6
- keys: bfloat16 [16384, 1024], P('ctx', 'tp'), may hold values from -6 to 6
- values: bfloat16 [16384, 1024], P('ctx', 'tp'), may hold values from -6 to 6
- out_weight: bfloat16 [5120, 4096], P('ctx', 'tp'), may hold values from -0.375 to 0.375
Outputs:
- mixed: bfloat16 [16384, 5120], P('ctx', 'tp')
The draws below stay inside these ranges and needn't reach their ends.
All inputs are finite; a program needn't handle non-finite values.
Results may differ from the reference program's by a relative error of at most 0.02.
Values may be sent and summed in bfloat16 or wider, within the bound.
A program may use at most 64 MiB of HBM per device.

```python
import math
import jax
import jax.numpy as jnp
from jax import lax

D = 5120
QH = 32
KVH = 8
HD = 128
TOKENS = 16384
HG = 512
N_TP = 8


def draw_queries(key, part):
    key = jax.random.fold_in(key, 1)
    return jnp.clip(2.0 * jax.random.normal(key, (TOKENS, QH * HD), jnp.float32), -6.0, 6.0).astype(jnp.bfloat16)


def draw_keys(key, part):
    key = jax.random.fold_in(key, 2)
    noise_key = jax.random.fold_in(key, 0)
    basis = jax.random.normal(noise_key, (TOKENS, KVH * HD), jnp.float32)
    return jnp.clip(basis, -6.0, 6.0).astype(jnp.bfloat16)


def steps_of(stream_key, shape, cuts, least, largest):
    level, own = 1.0, jax.random.fold_in(stream_key, 6)
    for dim, shards_of in cuts:
        draws = jnp.exp(jax.random.uniform(jax.random.fold_in(own, dim), (shards_of,), jnp.float32, least / len(cuts), largest / len(cuts)))
        level = level * jnp.repeat(draws, shape[dim] // shards_of).reshape([-1 if axis == dim else 1 for axis in range(len(shape))])
    return level


def scatter_about(stream_key, extent, spread, limit, cuts=(), kind=jnp.bfloat16):
    result = spread * jax.random.normal(stream_key, extent, jnp.float32)
    if cuts:
        result = result * steps_of(stream_key, extent, cuts, -0.22, 0.18)
    return jnp.clip(result, -limit, limit).astype(kind)


def setup_inputs(seed: int = 0) -> dict:
    key_of = jax.random.split(jax.random.key(seed), 5)
    queries = draw_queries(jax.random.fold_in(key_of[4], 71), 0)
    keys = draw_keys(jax.random.fold_in(key_of[4], 71), 0)
    values = scatter_about(key_of[2], (TOKENS, KVH * HD), 1.0, 6.0, ((0, 64), (1, 8)))
    out_weight = scatter_about(key_of[3], (D, QH * HD), (QH * HD // 16) ** -0.5, 0.375, ((0, 64), (1, 8)))
    return {"queries": queries, "keys": keys, "values": values, "out_weight": out_weight}


def rotate_heads(source, positions, head_count):
    half_width = HD // 2
    frequency = jnp.exp(-(jnp.arange(half_width, dtype=jnp.float32) / half_width) * math.log(1000000.0))
    angles = positions.astype(jnp.float32)[:, None] * frequency[None, :]
    cosine = jnp.cos(angles)[:, None, :]
    sines = jnp.sin(angles)[:, None, :]
    shaped = source.astype(jnp.float32).reshape(source.shape[0], head_count, HD)
    first_half = shaped[:, :, :half_width]
    second_half = shaped[:, :, half_width:]
    turned = jnp.concatenate([first_half * cosine - second_half * sines, second_half * cosine + first_half * sines], axis=2)
    return turned.reshape(source.shape[0], head_count * HD).astype(jnp.bfloat16)

def reference(queries, keys, values, out_weight):
    group_size = QH // KVH
    positions = jnp.arange(TOKENS, dtype=jnp.int32)
    query_rot = rotate_heads(queries, positions, QH).reshape(TOKENS, KVH, group_size, HD).astype(jnp.float32)
    key_rot = rotate_heads(keys, positions, KVH).reshape(TOKENS, KVH, HD).astype(jnp.float32)
    value_heads = values.reshape(TOKENS, KVH, HD).astype(jnp.float32)
    block_rows = math.gcd(TOKENS, 128)
    score_scale = 1.0 / math.sqrt(HD)

    def one_block(block_index):
        offset = (block_index * block_rows).astype(jnp.int32)
        query_block = lax.dynamic_slice_in_dim(query_rot, offset, block_rows, 0)
        scores = jnp.einsum('qkgd,nkd->kgqn', query_block, key_rot) * score_scale
        query_pos = offset + jnp.arange(block_rows, dtype=jnp.int32)
        visible = positions[None, :] <= query_pos[:, None]
        scores = jnp.where(visible, scores, -1e+30)
        maxima = lax.optimization_barrier(jnp.max(scores, axis=3, keepdims=True))
        unscaled = jnp.where(visible, jnp.exp(scores - maxima), 0.0)
        totals = lax.optimization_barrier(jnp.sum(unscaled, axis=3))
        weights = lax.optimization_barrier(unscaled.astype(jnp.bfloat16)).astype(jnp.float32)
        numerator = jnp.einsum('kgqn,nkd->qkgd', weights, value_heads)
        attended = numerator / jnp.transpose(totals, (2, 0, 1))[..., None]
        return attended.reshape(block_rows, QH * HD).astype(jnp.bfloat16)
    attended = lax.map(one_block, jnp.arange(TOKENS // block_rows, dtype=jnp.int32)).reshape(TOKENS, QH * HD)
    summed = jnp.zeros((TOKENS, D), jnp.float32)
    for group_index in range(N_TP):
        columns = slice(group_index * HG, (group_index + 1) * HG)
        partial_value = jnp.dot(attended[:, columns], out_weight[:, columns].T, preferred_element_type=jnp.float32)
        summed = summed + lax.optimization_barrier(partial_value.astype(jnp.bfloat16)).astype(jnp.float32)
    return summed.astype(jnp.bfloat16)
```

```python
import functools
import math

import jax
import jax.numpy as jnp
from jax import lax
from jax.experimental import pallas as pl
from jax.experimental.pallas import tpu as pltpu
from jax.sharding import PartitionSpec as P

HD = 128
NZ, NX, NH, NY, NC = 8, 4, 2, 4, 2
MESH = pl.DeviceIdType.MESH
LOW = -1e30


def rotate_heads(source, positions, head_count, head_width, scale):
    half_width = head_width // 2
    frequency = jnp.exp(
        -(jnp.arange(half_width, dtype=jnp.float32) / half_width) * math.log(1000000.0)
    )
    angles = positions.astype(jnp.float32)[:, None] * frequency[None, :]
    cosine = jnp.cos(angles)[:, None, :] * scale
    sines = jnp.sin(angles)[:, None, :] * scale
    shaped = source.astype(jnp.float32).reshape(source.shape[0], head_count, head_width)
    first_half = shaped[:, :, :half_width]
    second_half = shaped[:, :, half_width:]
    turned = jnp.concatenate(
        [first_half * cosine - second_half * sines, second_half * cosine + first_half * sines],
        axis=2,
    )
    return turned.reshape(source.shape[0], head_count * head_width).astype(jnp.bfloat16)


COUNT = 0


def numbers(*shape):
    global COUNT
    total = math.prod(shape)
    first = COUNT
    COUNT += total
    strides = [math.prod(shape[i + 1 :]) for i in range(len(shape))]
    return lambda *index: first + sum(i * s for i, s in zip(index, strides))


KV_H = numbers(1)
W_H = numbers(1)
Q_X = numbers(3)
KV_Z = numbers(2, 2, 4)
W_Z = numbers(2, 2, 4)
W_C = numbers(4)
O_X = numbers(3)
L_X = numbers(3)
A_X = numbers(3)
A_C = numbers(4)
Y_R = numbers(4, 4)
Y_L = numbers(4, 4)
F_X = numbers(3)


def kernel(
    q_ref, kv_ref, w_ref, out_ref,
    qbuf, kvbuf, wbuf, acc, mbuf, osend, orecv, lsend, lrecv, att, part,
    yleft, yright, ysend_r, ysend_l, fsend, frecv, ssem, rsem,
):
    rows = q_ref.shape[0]
    wrows = w_ref.shape[0]
    heads = q_ref.shape[1] // HD
    fw = NH * wrows
    ctx = lax.axis_index("ctx")
    tp = lax.axis_index("tp")
    z, x, h = ctx // (NX * NH), (ctx // NH) % NX, ctx % NH
    y, c = tp // NC, tp % NC

    def at(z=z, x=x, h=h, y=y, c=c):
        return (z * (NX * NH) + x * NH + h, y * NC + c)

    up, down = at(z=(z + 1) % NZ), at(z=(z + NZ - 1) % NZ)
    xs = [at(x=(x + d) % NX) for d in range(1, NX)]
    other_h, other_c = at(h=1 - h), at(c=1 - c)
    ring = h * NY + y
    y_next = (ring + 1) % (NH * NY)
    y_prev = (ring + NH * NY - 1) % (NH * NY)
    right = at(h=y_next // NY, y=y_next % NY)
    left = at(h=y_prev // NY, y=y_prev % NY)

    barrier = pltpu.get_barrier_semaphore()
    peers = [up, down, *xs, other_h, other_c, right, left]
    for peer in peers:
        pl.semaphore_signal(barrier, 1, device_id=peer, device_id_type=MESH)
    pl.semaphore_wait(barrier, len(peers))

    def copy(number, src, dst, peer):
        return pltpu.make_async_remote_copy(
            src_ref=src, dst_ref=dst, send_sem=ssem.at[number], recv_sem=rsem.at[number],
            device_id=peer, device_id_type=MESH,
        )

    sent = []

    def start(cp):
        cp.start()
        sent.append(cp)
        return cp

    def own_rows(n):
        return pl.ds(pl.multiple_of(h * n, 16), n)

    def other_rows(n):
        return pl.ds(pl.multiple_of((1 - h) * n, 16), n)

    halves = (own_rows, other_rows)

    def kv_z(direction, half, step):
        slot = (z + NZ - (step - 1)) % NZ if direction == 0 else (z + step - 1) % NZ
        ref = kvbuf.at[slot, halves[half](rows)]
        return copy(KV_Z(direction, half, step - 1), ref, ref, (up, down)[direction])

    def w_z(direction, half, step):
        slot = (z + NZ - (step - 1)) % NZ if direction == 0 else (z + step - 1) % NZ
        ref = wbuf.at[c, slot, halves[half](wrows)]
        return copy(W_Z(direction, half, step - 1), ref, ref, (up, down)[direction])

    def used(direction, half, step):
        return step <= 3 or (step == 4 and direction == half)

    kvh = start(copy(KV_H(0), kv_ref, kvbuf.at[z, own_rows(rows)], other_h))
    kvbuf[z, own_rows(rows)] = kv_ref[...]
    start(kv_z(0, 0, 1))
    start(kv_z(1, 0, 1))
    qx = [start(copy(Q_X(i), q_ref, qbuf.at[x], xs[i])) for i in (0, 2, 1)]
    wh = start(copy(W_H(0), w_ref, wbuf.at[c, z, own_rows(wrows)], other_h))
    wbuf[c, z, own_rows(wrows)] = w_ref[...]
    qbuf[x] = q_ref[...]
    acc[...] = jnp.zeros_like(acc)
    mbuf[...] = jnp.full_like(mbuf, LOW)

    def tile(place, slot, masked):
        keys = kvbuf[slot, :, 0:HD]
        vals = jnp.concatenate(
            [kvbuf[slot, :, HD : 2 * HD], jnp.ones((NH * rows, HD), jnp.bfloat16)], axis=1
        )
        for g in range(heads):
            query = qbuf[place, :, g * HD : (g + 1) * HD]
            s = lax.dot_general(
                query, keys, (((1,), (1,)), ((), ())), preferred_element_type=jnp.float32
            )
            if masked:
                key_pos = lax.broadcasted_iota(jnp.int32, s.shape, 1)
                row_pos = lax.broadcasted_iota(jnp.int32, s.shape, 0) + h * rows
                s = jnp.where(key_pos <= row_pos, s, LOW)
            old = mbuf[place, g]
            new = jnp.maximum(old, jnp.max(s, axis=1, keepdims=True))
            factor = jnp.exp2(old - new)
            p = jnp.exp2(s - jnp.concatenate([new] * (s.shape[1] // HD), axis=1))
            pv = jnp.dot(p.astype(jnp.bfloat16), vals, preferred_element_type=jnp.float32)
            mbuf[place, g] = new
            acc[place, g] = acc[place, g] * jnp.concatenate([factor] * 2, axis=1) + pv

    def attend(slot):
        @pl.loop(0, NX)
        def _(place):
            tile(place, slot, False)

    for cp in qx:
        cp.wait_recv()
    kvh.wait_recv()
    start(kv_z(0, 1, 1))
    start(kv_z(1, 1, 1))
    tile(x, z, True)

    @pl.loop(x + 1, NX)
    def _(place):
        tile(place, z, False)

    for step in range(1, 5):
        for half in range(2):
            for direction in range(2):
                if used(direction, half, step):
                    kv_z(direction, half, step).wait_recv()
                    if used(direction, half, step + 1):
                        start(kv_z(direction, half, step + 1))
        if step == 3:
            wh.wait_recv()
            for half in range(2):
                for direction in range(2):
                    start(w_z(direction, half, 1))

        @pl.when(z >= step)
        def _():
            attend((z + NZ - step) % NZ)

        if step < 4:
            @pl.when(z + step >= NZ)
            def _():
                attend((z + step) % NZ)

    def w_step(step):
        for half in range(2):
            for direction in range(2):
                if used(direction, half, step):
                    w_z(direction, half, step).wait_recv()
                    if used(direction, half, step + 1):
                        start(w_z(direction, half, step + 1))

    w_step(1)

    lane = lax.broadcasted_iota(jnp.int32, (rows, HD), 1)

    def finish(place):
        packed = jnp.full((rows, HD), LOW, jnp.float32)
        for g in range(heads):
            total = acc[place, g, :, HD : 2 * HD]
            some = total > 0.0
            safe = jnp.where(some, total, 1.0)
            osend[place, :, g * HD : (g + 1) * HD] = (
                acc[place, g, :, 0:HD] / safe
            ).astype(jnp.bfloat16)
            lse = jnp.where(some, mbuf[place, g] + jnp.log2(safe), LOW)
            packed = jnp.where(lane == g, lse, packed)
        lsend[place] = packed.T[0:8]

    ox, lx = [], []
    for d in (1, 3, 2):
        place = (x + d) % NX
        finish(place)
        ox.append(start(copy(O_X(d - 1), osend.at[place], orecv.at[x], xs[d - 1])))
        lx.append(start(copy(L_X(d - 1), lsend.at[place], lrecv.at[x], xs[d - 1])))
    finish(x)
    orecv[x] = osend[x]
    lrecv[x] = lsend[x]
    w_step(2)
    for cp in ox + lx:
        cp.wait_recv()
    lses = [lrecv[i] for i in range(NX)]
    top = functools.reduce(jnp.maximum, lses)
    shares = [jnp.exp2(v - top) for v in lses]
    whole = sum(shares)
    shares = [v / whole for v in shares]
    shares.append(jnp.zeros((HD - 8 * NX, rows), jnp.float32))
    turned = jnp.concatenate(shares, axis=0).T
    for g in range(heads):
        total = jnp.zeros((rows, HD), jnp.float32)
        for i in range(NX):
            column = turned[:, 8 * i + g : 8 * i + g + 1]
            total += column * orecv[i, :, g * HD : (g + 1) * HD].astype(jnp.float32)
        att[c, x, :, g * HD : (g + 1) * HD] = total.astype(jnp.bfloat16)

    ax = [start(copy(A_X(i), att.at[c, x], att.at[c, x], xs[i])) for i in (0, 2, 1)]
    ac = [start(copy(A_C(0), att.at[c, x], att.at[c, x], other_c))]
    w_step(3)
    w_step(4)
    wc = []
    for i in range(NZ // 2):
        ref = wbuf.at[c, 2 * i + 1 - c]
        wc.append(start(copy(W_C(i), ref, ref, other_c)))
    for n, i in enumerate((0, 2, 1)):
        ax[n].wait_recv()
        ref = att.at[c, (x + NX - 1 - i) % NX]
        ac.append(start(copy(A_C(1 + n), ref, ref, other_c)))
    for cp in ac + wc:
        cp.wait_recv()

    @pl.loop(0, NY)
    def _(dest):
        @pl.loop(0, NX)
        def _(place):
            total = jnp.zeros((fw, rows), jnp.float32)
            for col in range(NC):
                total += lax.dot_general(
                    wbuf[col, 2 * dest + c], att[col, place],
                    (((1,), (1,)), ((), ())), preferred_element_type=jnp.float32,
                )
            part[dest, place] = total

    def y_right(turn, dest):
        place = (x + 1 + turn) % NX
        return copy(
            Y_R(turn, dest), ysend_r.at[dest, place], yleft.at[dest, place], right
        )

    def y_left(turn, dest):
        place = (x + 1 + turn) % NX
        return copy(
            Y_L(turn, dest), ysend_l.at[dest, place], yright.at[dest, place], left
        )

    fx = []
    for turn in range(NX):
        place = (x + 1 + turn) % NX
        for i in range(NY - 1):
            dest = NY - 1 - i

            @pl.when(y == 0)
            def _():
                ysend_r[dest, place] = part[dest, place].astype(jnp.bfloat16)
                y_right(turn, dest).start()

            dest_l = i

            @pl.when(y == NY - 1)
            def _():
                ysend_l[dest_l, place] = part[dest_l, place].astype(jnp.bfloat16)
                y_left(turn, dest_l).start()

    for turn in range(NX):
        place = (x + 1 + turn) % NX
        for i in range(NY - 1):
            dest = NY - 1 - i

            @pl.when((y > 0) & (y < dest))
            def _():
                y_right(turn, dest).wait_recv()
                ysend_r[dest, place] = (
                    part[dest, place] + yleft[dest, place].astype(jnp.float32)
                ).astype(jnp.bfloat16)
                y_right(turn, dest).start()

            dest_l = i

            @pl.when((y < NY - 1) & (y > dest_l))
            def _():
                y_left(turn, dest_l).wait_recv()
                ysend_l[dest_l, place] = (
                    part[dest_l, place] + yright[dest_l, place].astype(jnp.float32)
                ).astype(jnp.bfloat16)
                y_left(turn, dest_l).start()

        for dest in range(NY):

            @pl.when(y == dest)
            def _():
                total = part[dest, place]
                if dest > 0:
                    y_right(turn, dest).wait_recv()
                    total += yleft[dest, place].astype(jnp.float32)
                if dest < NY - 1:
                    y_left(turn, dest).wait_recv()
                    total += yright[dest, place].astype(jnp.float32)
                fsend[place] = total.astype(jnp.bfloat16)

        if turn < NX - 1:
            fx.append(start(copy(F_X(turn), fsend.at[place], frecv.at[x], xs[turn])))
    frecv[x] = fsend[x]
    for cp in fx:
        cp.wait_recv()
    for i in range(NX):
        out_ref[i * fw : (i + 1) * fw] = frecv[i]

    for cp in sent:
        cp.wait_send()
    for turn in range(NX):
        for dest in range(NY):

            @pl.when(y < dest)
            def _():
                y_right(turn, dest).wait_send()

            @pl.when(y > dest)
            def _():
                y_left(turn, dest).wait_send()


def body(queries, keys, values, out_weight):
    rows = queries.shape[0]
    wrows = out_weight.shape[0]
    cols = queries.shape[1]
    heads = cols // HD
    fw = NH * wrows
    positions = lax.axis_index("ctx") * rows + jnp.arange(rows, dtype=jnp.int32)
    scale = math.log2(math.e) / math.sqrt(HD)
    query_rot = rotate_heads(queries, positions, heads, HD, scale)
    key_rot = rotate_heads(keys, positions, keys.shape[1] // HD, HD, 1.0)
    key_value = jnp.concatenate([key_rot, values], axis=1)
    vmem = pl.BlockSpec(memory_space=pltpu.VMEM)
    bf16, f32 = jnp.bfloat16, jnp.float32
    turned = pl.pallas_call(
        kernel,
        out_shape=jax.ShapeDtypeStruct((NX * fw, rows), bf16),
        in_specs=[vmem] * 3,
        out_specs=vmem,
        scratch_shapes=[
            pltpu.VMEM((NX, rows, cols), bf16),
            pltpu.VMEM((NZ, NH * rows, 2 * HD), bf16),
            pltpu.VMEM((NC, NZ, fw, cols), bf16),
            pltpu.VMEM((NX, heads, rows, 2 * HD), f32),
            pltpu.VMEM((NX, heads, rows, HD), f32),
            pltpu.VMEM((NX, rows, cols), bf16),
            pltpu.VMEM((NX, rows, cols), bf16),
            pltpu.VMEM((NX, 8, rows), f32),
            pltpu.VMEM((NX, 8, rows), f32),
            pltpu.VMEM((NC, NX, rows, cols), bf16),
            pltpu.VMEM((NY, NX, fw, rows), f32),
            pltpu.VMEM((NY, NX, fw, rows), bf16),
            pltpu.VMEM((NY, NX, fw, rows), bf16),
            pltpu.VMEM((NY, NX, fw, rows), bf16),
            pltpu.VMEM((NY, NX, fw, rows), bf16),
            pltpu.VMEM((NX, fw, rows), bf16),
            pltpu.VMEM((NX, fw, rows), bf16),
            pltpu.SemaphoreType.DMA((COUNT,)),
            pltpu.SemaphoreType.DMA((COUNT,)),
        ],
        compiler_params=pltpu.CompilerParams(
            collective_id=0, has_side_effects=True, vmem_limit_bytes=56 * 2**20
        ),
        name="attention_layer",
    )(query_rot, key_value, out_weight)
    return turned.T


def solution(mesh):
    placed = (P("ctx", "tp"), P("ctx", "tp"), P("ctx", "tp"), P("ctx", "tp"))
    return jax.shard_map(
        body, mesh=mesh, in_specs=placed, out_specs=P("ctx", "tp"), check_vma=False
    )
```

```python
import functools
import math

import jax
import jax.numpy as jnp
from jax import lax
from jax.experimental import pallas as pl
from jax.experimental.pallas import tpu as pltpu
from jax.sharding import PartitionSpec as P

HD = 128
NZ, NX, NH, NY, NC = 8, 4, 2, 4, 2
NS = 4
NU = 2
MESH = pl.DeviceIdType.MESH
LOW = -1e30


def rotation(positions):
    half_width = HD // 2
    frequency = jnp.exp(
        -(jnp.arange(half_width, dtype=jnp.float32) / half_width) * math.log(1000000.0)
    )
    angles = positions.astype(jnp.float32)[:, None] * frequency[None, :]
    cosine = jnp.cos(angles)
    sines = jnp.sin(angles)
    return jnp.concatenate([cosine, cosine], axis=1), jnp.concatenate([-sines, sines], axis=1)


COUNT = 0


def numbers(*shape):
    global COUNT
    total = math.prod(shape)
    first = COUNT
    COUNT += total
    strides = [math.prod(shape[i + 1 :]) for i in range(len(shape))]
    return lambda *index: first + sum(i * s for i, s in zip(index, strides))


KV_H = numbers(NU)
W_H = numbers(2, 5)
Q_X = numbers(NS, 3)
KV_Z = numbers(2, 2, 4, NU)
W_Z = numbers(2, 4)
W_C = numbers(4)
O_X = numbers(NS, 3)
L_X = numbers(NS, 3)
A_X = numbers(NS, 3)
A_C = numbers(NS, 4)
Y_R = numbers(NS, 4)
Y_L = numbers(NS, 4)
F_X = numbers(NS // 2, 3)


def kernel(
    q_ref, k_ref, v_ref, w_ref, cos_ref, sin_ref, out_ref,
    qbuf, kvbuf, wbuf, acc, mbuf, osend, orecv, lsend, lrecv, att, part,
    yleft, yright, ysend_r, ysend_l, fsum, fsend, frecv, ssem, rsem,
):
    rows = q_ref.shape[0]
    wrows = w_ref.shape[0]
    heads = q_ref.shape[1] // HD
    fw = NH * wrows
    some_rows = rows // NS
    ctx = lax.axis_index("ctx")
    tp = lax.axis_index("tp")
    z, x, h = ctx // (NX * NH), (ctx // NH) % NX, ctx % NH
    y, c = tp // NC, tp % NC

    def at(z=z, x=x, h=h, y=y, c=c):
        return (z * (NX * NH) + x * NH + h, y * NC + c)

    up, down = at(z=(z + 1) % NZ), at(z=(z + NZ - 1) % NZ)
    xs = [at(x=(x + d) % NX) for d in range(1, NX)]
    other_h, other_c = at(h=1 - h), at(c=1 - c)
    ring = h * NY + y
    y_next = (ring + 1) % (NH * NY)
    y_prev = (ring + NH * NY - 1) % (NH * NY)
    right = at(h=y_next // NY, y=y_next % NY)
    left = at(h=y_prev // NY, y=y_prev % NY)

    across = at(y=(y + 2) % NY)

    barrier = pltpu.get_barrier_semaphore()
    peers = [other_h, up, down, *xs, across, right, left, other_c]
    for peer in peers:
        pl.semaphore_signal(barrier, 1, device_id=peer, device_id_type=MESH)

    def copy(number, src, dst, peer):
        return pltpu.make_async_remote_copy(
            src_ref=src, dst_ref=dst, send_sem=ssem.at[number], recv_sem=rsem.at[number],
            device_id=peer, device_id_type=MESH,
        )

    def own_rows(n):
        return pl.ds(pl.multiple_of(h * n, 16), n)

    def rotated(source):
        wide = source.astype(jnp.float32)
        return wide * cos_ref[...] + pltpu.roll(wide, HD // 2, 1) * sin_ref[...]

    def slot_of(direction, step):
        return (z + NZ - (step - 1)) % NZ if direction == 0 else (z + step - 1) % NZ

    piece = rows // NU

    def kv_rows(half, u):
        first = h * rows if half == 0 else (1 - h) * rows
        return pl.ds(pl.multiple_of(first + u * piece, piece), piece)

    def kv_h(u):
        ref = kvbuf.at[z, kv_rows(0, u)]
        return copy(KV_H(u), ref, ref, other_h)

    def kv_z(direction, half, step, u):
        ref = kvbuf.at[slot_of(direction, step), kv_rows(half, u)]
        return copy(KV_Z(direction, half, step - 1, u), ref, ref, (up, down)[direction])

    def w_z(direction, step):
        ref = wbuf.at[c, slot_of(direction, step), own_rows(wrows)]
        return copy(W_Z(direction, step - 1), ref, ref, (up, down)[direction])

    def w_h(direction, step):
        ref = wbuf.at[c, slot_of(direction, step + 1), own_rows(wrows)]
        return copy(W_H(direction, step), ref, ref, other_h)

    def w_c(i):
        ref = wbuf.at[c, 2 * i + 1 - c]
        return copy(W_C(i), ref, ref, other_c)

    def part_rows(s):
        return pl.ds(pl.multiple_of(s * some_rows, some_rows), some_rows)

    def q_x(s, i):
        ref = qbuf.at[x, part_rows(s)]
        return copy(Q_X(s, i), ref, ref, xs[i])

    def when(condition, action):
        if condition is True:
            action()
        elif condition is not False:
            pl.when(condition)(action)

    def pass_on(half, step):
        last = 4 if half == 0 else 3
        for u in range(NU):
            for direction in range(2):
                steps = last if direction == 0 else 7 - last
                here = functools.partial(kv_z, direction, half, step, u)
                there = functools.partial(kv_z, direction, half, step + 1, u)
                when(step <= steps, lambda: here().wait_recv())
                when(step < steps, lambda: there().start())

    def w_step(step):
        for direction in range(2):
            steps = 4 - direction
            when(step <= steps, lambda: w_z(direction, step).wait_recv())
            when(step < steps, lambda: w_z(direction, step + 1).start())
            when(step <= steps, lambda: w_h(direction, step).start())

    kvbuf[z, own_rows(rows), 0:HD] = rotated(k_ref[...]).astype(jnp.bfloat16)
    kvbuf[z, own_rows(rows), HD : 2 * HD] = v_ref[...]
    scale = math.log2(math.e) / math.sqrt(HD)
    for g in range(heads):
        cols = slice(g * HD, (g + 1) * HD)
        qbuf[x, :, cols] = (rotated(q_ref[:, cols]) * scale).astype(jnp.bfloat16)
    wbuf[c, z, own_rows(wrows)] = w_ref[...]
    pl.semaphore_wait(barrier, len(peers))

    for u in range(NU):
        kv_h(u).start()
    for u in range(NU):
        for direction in range(2):
            kv_z(direction, 0, 1, u).start()

    @pl.loop(0, NS)
    def _(s):
        for i in (0, 2, 1):
            q_x(s, i).start()

    w_h(0, 0).start()
    w_z(0, 1).start()
    w_z(1, 1).start()
    acc[...] = jnp.zeros_like(acc)
    mbuf[...] = jnp.full_like(mbuf, LOW)

    def tile(place, s, slots, masked):
        count = NH * rows
        query = jnp.concatenate(
            [qbuf[place, part_rows(s), g * HD : (g + 1) * HD] for g in range(heads)], axis=0
        )
        scores = []
        for slot in slots:
            scores.append(
                lax.dot_general(
                    query, kvbuf[slot, :, 0:HD],
                    (((1,), (1,)), ((), ())), preferred_element_type=jnp.float32,
                )
            )
        if masked:
            key_pos = lax.broadcasted_iota(jnp.int32, scores[0].shape, 1)
            row_pos = lax.broadcasted_iota(jnp.int32, scores[0].shape, 0) % some_rows
            seen = key_pos <= row_pos + (h * rows + s * some_rows)
            scores = [jnp.where(seen, v, LOW) for v in scores]
        old = mbuf[place, s]
        new = old
        for v in scores:
            new = jnp.maximum(new, jnp.max(v, axis=1, keepdims=True))
        factor = jnp.exp2(old - new)
        wide = jnp.concatenate([new] * (count // HD), axis=1)
        total = acc[place, s] * jnp.concatenate([factor] * 2, axis=1)
        for slot, v in zip(slots, scores):
            vals = jnp.concatenate(
                [kvbuf[slot, :, HD : 2 * HD], jnp.ones((count, HD), jnp.bfloat16)], axis=1
            )
            total += jnp.dot(
                jnp.exp2(v - wide).astype(jnp.bfloat16), vals, preferred_element_type=jnp.float32
            )
        mbuf[place, s] = new
        acc[place, s] = total

    def attend(s, step):
        lower, upper = (z + NZ - step) % NZ, (z + step) % NZ
        both = (z + step >= NZ) & (step < NZ // 2)

        @pl.when(both)
        def _():
            for place in range(NX):
                tile(place, s, (lower, upper), False)

        @pl.when(jnp.logical_not(both) & (z >= step))
        def _():
            for place in range(NX):
                tile(place, s, (lower,), False)

    pass_on(0, 1)
    for u in range(NU):
        kv_h(u).wait_recv()
        for direction in range(2):
            kv_z(direction, 1, 1, u).start()

    @pl.loop(0, NS)
    def _(s):
        for i in range(NX - 1):
            q_x(s, i).wait_recv()
        tile(x, s, (z,), True)

        @pl.loop(x + 1, NX)
        def _(place):
            tile(place, s, (z,), False)

        @pl.when(s == 1)
        def _():
            pass_on(0, 2)

    @pl.loop(1, 4)
    def _(step):
        pass_on(1, step)

        @pl.loop(0, NS)
        def _(s):
            attend(s, step)

            @pl.when((s == 0) & (step < 3))
            def _():
                pass_on(0, step + 2)

            @pl.when(s == 1)
            def _():
                w_step(step)

    pass_on(1, 4)
    w_step(4)

    def finish(place, s):
        total = acc[place, s, :, HD : 2 * HD]
        some = total > 0.0
        safe = jnp.where(some, total, 1.0)
        osend[s, place] = (acc[place, s, :, 0:HD] / safe).astype(jnp.bfloat16)
        lse = jnp.where(some, mbuf[place, s] + jnp.log2(safe), LOW)
        lsend[s, place] = lse.T[0:8]

    def l_x(s, d):
        place = (x + 1 + d) % NX
        return copy(L_X(s, d), lsend.at[s, place], lrecv.at[s, x], xs[d])

    def o_x(s, d):
        place = (x + 1 + d) % NX
        return copy(O_X(s, d), osend.at[s, place], orecv.at[s, x], xs[d])

    def send_shares(s):
        for d in (0, 2, 1):
            finish((x + 1 + d) % NX, s)
            l_x(s, d).start()
            o_x(s, d).start()
        finish(x, s)
        orecv[s, x] = osend[s, x]
        lrecv[s, x] = lsend[s, x]

    def a_x(s, i):
        ref = att.at[c, s, x]
        return copy(A_X(s, i), ref, ref, xs[i])

    def a_c(s, n):
        ref = att.at[c, s, (x + NX - n) % NX]
        return copy(A_C(s, n), ref, ref, other_c)

    def combine(s):
        for d in range(NX - 1):
            l_x(s, d).wait_recv()
            o_x(s, d).wait_recv()
        lses = [lrecv[s, i] for i in range(NX)]
        top = functools.reduce(jnp.maximum, lses)
        shares = [jnp.exp2(v - top) for v in lses]
        whole = sum(shares)
        shares = [v / whole for v in shares]
        shares.append(jnp.zeros((HD - 8 * NX, heads * some_rows), jnp.float32))
        turned = jnp.concatenate(shares, axis=0).T
        total = jnp.zeros((heads * some_rows, HD), jnp.float32)
        for i in range(NX):
            total += turned[:, 8 * i : 8 * i + 1] * orecv[s, i].astype(jnp.float32)
        total = total.astype(jnp.bfloat16)
        for g in range(heads):
            att[c, s, x, :, g * HD : (g + 1) * HD] = total[g * some_rows : (g + 1) * some_rows]
        for i in (0, 2, 1):
            a_x(s, i).start()
        a_c(s, 0).start()

    def gather(s):
        for i in (0, 2, 1):
            a_x(s, i).wait_recv()
            a_c(s, i + 1).start()

    def y_right(s, slot, peer):
        return copy(Y_R(s, slot), ysend_r.at[s, slot], yleft.at[s, slot], peer)

    def y_left(s, slot, peer):
        return copy(Y_L(s, slot), ysend_l.at[s, slot], yright.at[s, slot], peer)

    def put_right(s, slot, value, peer):
        ysend_r[s, slot] = value.astype(jnp.bfloat16)
        y_right(s, slot, peer).start()

    def put_left(s, slot, value, peer):
        ysend_l[s, slot] = value.astype(jnp.bfloat16)
        y_left(s, slot, peer).start()

    def project(s):
        for n in range(NX):
            a_c(s, n).wait_recv()
        mixed = [att[col, s].reshape(NX * some_rows, heads * HD) for col in range(NC)]

        @pl.loop(0, NY)
        def _(dest):
            total = jnp.zeros((fw, NX * some_rows), jnp.float32)
            for col in range(NC):
                total += lax.dot_general(
                    wbuf[col, 2 * dest + c], mixed[col],
                    (((1,), (1,)), ((), ())), preferred_element_type=jnp.float32,
                )
            part[s, dest] = total

        @pl.when(y == 0)
        def _():
            for dest in (3, 2, 1):
                put_right(s, dest, part[s, dest], right)

        @pl.when(y == 1)
        def _():
            put_left(s, 3, part[s, 0], left)

        @pl.when(y == 2)
        def _():
            put_right(s, 0, part[s, 3], right)

        @pl.when(y == 3)
        def _():
            for dest in (0, 1, 2):
                put_left(s, dest, part[s, dest], left)

    def sum_on(s):
        @pl.when(y == 1)
        def _():
            for dest, peer in ((3, across), (2, right)):
                y_right(s, dest, peer).wait_recv()
                put_right(s, dest, part[s, dest] + yleft[s, dest].astype(jnp.float32), peer)

        @pl.when(y == 2)
        def _():
            for dest, peer in ((0, across), (1, left)):
                y_left(s, dest, peer).wait_recv()
                put_left(s, dest, part[s, dest] + yright[s, dest].astype(jnp.float32), peer)

    def sum_up(s):
        @pl.when(y == 0)
        def _():
            y_left(s, 3, left).wait_recv()
            y_left(s, 0, across).wait_recv()
            fsum[s] = (
                part[s, 0] + yright[s, 3].astype(jnp.float32) + yright[s, 0].astype(jnp.float32)
            )

        @pl.when(y == 3)
        def _():
            y_right(s, 0, right).wait_recv()
            y_right(s, 3, across).wait_recv()
            fsum[s] = (
                part[s, 3] + yleft[s, 0].astype(jnp.float32) + yleft[s, 3].astype(jnp.float32)
            )

        for middle in (1, 2):

            @pl.when(y == middle)
            def _():
                y_right(s, middle, right).wait_recv()
                y_left(s, middle, left).wait_recv()
                fsum[s] = (
                    part[s, middle]
                    + yleft[s, middle].astype(jnp.float32)
                    + yright[s, middle].astype(jnp.float32)
                )

    def f_x(pair, d):
        place = (x + 1 + d) % NX
        return copy(F_X(pair, d), fsend.at[pair, place], frecv.at[pair, x], xs[d])

    def deliver(pair):
        first, second = fsum[2 * pair], fsum[2 * pair + 1]
        for place in range(NX):
            cols = slice(place * some_rows, (place + 1) * some_rows)
            both = jnp.concatenate([first[:, cols], second[:, cols]], axis=1)
            fsend[pair, place] = both.astype(jnp.bfloat16)
        for d in (0, 2, 1):
            f_x(pair, d).start()
        frecv[pair, x] = fsend[pair, x]

    def store(pair):
        for d in range(NX - 1):
            f_x(pair, d).wait_recv()
        whole = frecv[pair].reshape(NX * fw, 2 * some_rows).astype(jnp.float32)
        tokens = pl.ds(pl.multiple_of(pair * 2 * some_rows, 2 * some_rows), 2 * some_rows)
        out_ref[tokens] = whole.T.astype(jnp.bfloat16)

    def stage(turn, late, action, count=NS):
        pl.when((turn >= late) & (turn < late + count))(lambda: action(turn - late))

    @pl.loop(0, NS + 4)
    def _(turn):
        @pl.when(turn < NS)
        def _():
            @pl.when(z >= 4)
            def _():
                for place in range(NX):
                    tile(place, turn, ((z + NZ - 4) % NZ,), False)

            send_shares(turn)

        @pl.when(turn == 1)
        def _():
            for direction in range(2):
                for step in range(5 - direction):
                    if step > 0 or direction == 0:
                        w_h(direction, step).wait_recv()
            for i in range(NZ // 2):
                w_c(i).start()

        @pl.when(turn == 2)
        def _():
            for i in range(NZ // 2):
                w_c(i).wait_recv()

        stage(turn, 1, combine)
        stage(turn, 2, gather)
        stage(turn, 2, project)
        stage(turn, 3, sum_on)
        stage(turn, 4, sum_up)

        @pl.when((turn == 5) | (turn == 7))
        def _():
            deliver((turn - 5) // 2)

    for pair in range(NS // 2):
        store(pair)

    for u in range(NU):
        kv_h(u).wait_send()
        for direction in range(2):
            for half in range(2):
                for step in range(1, 5):
                    if step < 4 or direction == half:
                        kv_z(direction, half, step, u).wait_send()
    for direction in range(2):
        for step in range(1, 5 - direction):
            w_z(direction, step).wait_send()
        for step in range(direction, 5 - direction):
            w_h(direction, step).wait_send()
    for i in range(NZ // 2):
        w_c(i).wait_send()
    for pair in range(NS // 2):
        for d in range(NX - 1):
            f_x(pair, d).wait_send()

    @pl.loop(0, NS)
    def _(s):
        for d in range(NX - 1):
            q_x(s, d).wait_send()
            l_x(s, d).wait_send()
            o_x(s, d).wait_send()
            a_x(s, d).wait_send()
        for n in range(NX):
            a_c(s, n).wait_send()

        @pl.when(y == 0)
        def _():
            for dest in (3, 2, 1):
                y_right(s, dest, right).wait_send()

        @pl.when(y == 1)
        def _():
            y_left(s, 3, left).wait_send()
            y_right(s, 3, across).wait_send()
            y_right(s, 2, right).wait_send()

        @pl.when(y == 2)
        def _():
            y_right(s, 0, right).wait_send()
            y_left(s, 0, across).wait_send()
            y_left(s, 1, left).wait_send()

        @pl.when(y == 3)
        def _():
            for dest in (0, 1, 2):
                y_left(s, dest, left).wait_send()


def body(queries, keys, values, out_weight):
    rows = queries.shape[0]
    wrows = out_weight.shape[0]
    cols = queries.shape[1]
    heads = cols // HD
    fw = NH * wrows
    some = rows // NS
    positions = lax.axis_index("ctx") * rows + jnp.arange(rows, dtype=jnp.int32)
    cosine, sines = rotation(positions)
    vmem = pl.BlockSpec(memory_space=pltpu.VMEM)
    bf16, f32 = jnp.bfloat16, jnp.float32
    return pl.pallas_call(
        kernel,
        out_shape=jax.ShapeDtypeStruct((rows, NX * fw), bf16),
        in_specs=[vmem] * 6,
        out_specs=vmem,
        scratch_shapes=[
            pltpu.VMEM((NX, rows, cols), bf16),
            pltpu.VMEM((NZ, NH * rows, 2 * HD), bf16),
            pltpu.VMEM((NC, NZ, fw, cols), bf16),
            pltpu.VMEM((NX, NS, heads * some, 2 * HD), f32),
            pltpu.VMEM((NX, NS, heads * some, HD), f32),
            pltpu.VMEM((NS, NX, heads * some, HD), bf16),
            pltpu.VMEM((NS, NX, heads * some, HD), bf16),
            pltpu.VMEM((NS, NX, 8, heads * some), f32),
            pltpu.VMEM((NS, NX, 8, heads * some), f32),
            pltpu.VMEM((NC, NS, NX, some, cols), bf16),
            pltpu.VMEM((NS, NY, fw, NX * some), f32),
            pltpu.VMEM((NS, NY, fw, NX * some), bf16),
            pltpu.VMEM((NS, NY, fw, NX * some), bf16),
            pltpu.VMEM((NS, NY, fw, NX * some), bf16),
            pltpu.VMEM((NS, NY, fw, NX * some), bf16),
            pltpu.VMEM((NS, fw, NX * some), f32),
            pltpu.VMEM((NS // 2, NX, fw, 2 * some), bf16),
            pltpu.VMEM((NS // 2, NX, fw, 2 * some), bf16),
            pltpu.SemaphoreType.DMA((COUNT,)),
            pltpu.SemaphoreType.DMA((COUNT,)),
        ],
        compiler_params=pltpu.CompilerParams(
            collective_id=0, has_side_effects=True, vmem_limit_bytes=56 * 2**20
        ),
        name="attention_layer",
    )(queries, keys, values, out_weight, cosine, sines)


def solution(mesh):
    placed = (P("ctx", "tp"), P("ctx", "tp"), P("ctx", "tp"), P("ctx", "tp"))
    return jax.shard_map(
        body, mesh=mesh, in_specs=placed, out_specs=P("ctx", "tp"), check_vma=False
    )
```

```python
import functools
import math

import jax
import jax.numpy as jnp
from jax import lax
from jax.experimental import pallas as pl
from jax.experimental.pallas import tpu as pltpu
from jax.sharding import PartitionSpec as P

HD = 128
NZ, NX, NH, NY, NC = 8, 4, 2, 4, 2
NS = 4
NU = 2
MESH = pl.DeviceIdType.MESH
LOW = -1e30


def rotation(positions):
    half_width = HD // 2
    frequency = jnp.exp(
        -(jnp.arange(half_width, dtype=jnp.float32) / half_width) * math.log(1000000.0)
    )
    angles = positions.astype(jnp.float32)[:, None] * frequency[None, :]
    cosine = jnp.cos(angles)
    sines = jnp.sin(angles)
    return cosine, sines


COUNT = 0


def numbers(*shape):
    global COUNT
    total = math.prod(shape)
    first = COUNT
    COUNT += total
    strides = [math.prod(shape[i + 1 :]) for i in range(len(shape))]
    return lambda *index: first + sum(i * s for i, s in zip(index, strides))


KV_H = numbers(NU)
W_H = numbers(2, 5)
Q_X = numbers(NS, 3)
KV_Z = numbers(2, 2, 4, NU)
W_Z = numbers(2, 4)
W_C = numbers(4)
O_X = numbers(NS, 3)
L_X = numbers(NS, 3)
A_X = numbers(NS, 3)
A_C = numbers(NS, 4)
Y_R = numbers(NS, 4)
Y_L = numbers(NS, 4)
F_X = numbers(NS // 2, 3)


def kernel(
    q_ref, k_ref, v_ref, w_ref, cos_ref, sin_ref, out_ref,
    qbuf, kvbuf, wbuf, acc, mbuf, osend, orecv, lsend, lrecv, att, part,
    yleft, yright, ysend_r, ysend_l, fsum, fsend, frecv, ssem, rsem,
):
    rows = q_ref.shape[0]
    wrows = w_ref.shape[0]
    heads = q_ref.shape[1] // HD
    fw = NH * wrows
    some_rows = rows // NS
    ctx = lax.axis_index("ctx")
    tp = lax.axis_index("tp")
    z, x, h = ctx // (NX * NH), (ctx // NH) % NX, ctx % NH
    y, c = tp // NC, tp % NC

    def at(z=z, x=x, h=h, y=y, c=c):
        return (z * (NX * NH) + x * NH + h, y * NC + c)

    up, down = at(z=(z + 1) % NZ), at(z=(z + NZ - 1) % NZ)
    xs = [at(x=(x + d) % NX) for d in range(1, NX)]
    other_h, other_c = at(h=1 - h), at(c=1 - c)
    ring = h * NY + y
    y_next = (ring + 1) % (NH * NY)
    y_prev = (ring + NH * NY - 1) % (NH * NY)
    right = at(h=y_next // NY, y=y_next % NY)
    left = at(h=y_prev // NY, y=y_prev % NY)

    across = at(y=(y + 2) % NY)

    barrier = pltpu.get_barrier_semaphore()
    peers = [other_h, up, down, *xs, across, right, left, other_c]
    for peer in peers:
        pl.semaphore_signal(barrier, 1, device_id=peer, device_id_type=MESH)

    def copy(number, src, dst, peer):
        return pltpu.make_async_remote_copy(
            src_ref=src, dst_ref=dst, send_sem=ssem.at[number], recv_sem=rsem.at[number],
            device_id=peer, device_id_type=MESH,
        )

    def own_rows(n):
        return pl.ds(pl.multiple_of(h * n, 16), n)

    cosine = jnp.concatenate([cos_ref[...], cos_ref[...]], axis=1)
    sines = jnp.concatenate([-sin_ref[...], sin_ref[...]], axis=1)

    def rotated(source):
        wide = source.astype(jnp.float32)
        return wide * cosine + pltpu.roll(wide, HD // 2, 1) * sines

    def slot_of(direction, step):
        return (z + NZ - (step - 1)) % NZ if direction == 0 else (z + step - 1) % NZ

    piece = rows // NU

    def kv_rows(half, u):
        first = h * rows if half == 0 else (1 - h) * rows
        return pl.ds(pl.multiple_of(first + u * piece, piece), piece)

    def kv_h(u):
        ref = kvbuf.at[z, kv_rows(0, u)]
        return copy(KV_H(u), ref, ref, other_h)

    def kv_z(direction, half, step, u):
        ref = kvbuf.at[slot_of(direction, step), kv_rows(half, u)]
        return copy(KV_Z(direction, half, step - 1, u), ref, ref, (up, down)[direction])

    def w_at(slot):
        return wbuf.at[c, slot % 2, slot // 2, own_rows(wrows)]

    def w_z(direction, step):
        ref = w_at(slot_of(direction, step))
        return copy(W_Z(direction, step - 1), ref, ref, (up, down)[direction])

    def w_h(direction, step):
        ref = w_at(slot_of(direction, step + 1))
        return copy(W_H(direction, step), ref, ref, other_h)

    def w_c(i):
        ref = wbuf.at[c, 1 - c, i]
        return copy(W_C(i), ref, ref, other_c)

    def part_rows(s):
        return pl.ds(pl.multiple_of(s * some_rows, some_rows), some_rows)

    def q_x(s, i):
        ref = qbuf.at[x, part_rows(s)]
        return copy(Q_X(s, i), ref, ref, xs[i])

    def when(condition, action):
        if condition is True:
            action()
        elif condition is not False:
            pl.when(condition)(action)

    def pass_on(half, step):
        last = 4 if half == 0 else 3
        for u in range(NU):
            for direction in range(2):
                steps = last if direction == 0 else 7 - last
                here = functools.partial(kv_z, direction, half, step, u)
                there = functools.partial(kv_z, direction, half, step + 1, u)
                when(step <= steps, lambda: here().wait_recv())
                when(step < steps, lambda: there().start())

    def w_step(step):
        for direction in range(2):
            steps = 4 - direction
            when(step <= steps, lambda: w_z(direction, step).wait_recv())
            when(step < steps, lambda: w_z(direction, step + 1).start())
            when(step <= steps, lambda: w_h(direction, step).start())

    kvbuf[z, own_rows(rows), 0:HD] = rotated(k_ref[...]).astype(jnp.bfloat16)
    kvbuf[z, own_rows(rows), HD : 2 * HD] = v_ref[...]
    scale = math.log2(math.e) / math.sqrt(HD)
    for g in range(heads):
        cols = slice(g * HD, (g + 1) * HD)
        qbuf[x, :, cols] = (rotated(q_ref[:, cols]) * scale).astype(jnp.bfloat16)
    wbuf[c, z % 2, z // 2, own_rows(wrows)] = w_ref[...]
    pl.semaphore_wait(barrier, len(peers))

    for u in range(NU):
        kv_h(u).start()
    for u in range(NU):
        for direction in range(2):
            kv_z(direction, 0, 1, u).start()

    w_z(0, 1).start()
    w_z(1, 1).start()

    @pl.loop(0, NS)
    def _(s):
        for i in (0, 2, 1):
            q_x(s, i).start()

    acc[...] = jnp.zeros_like(acc)
    mbuf[...] = jnp.full_like(mbuf, LOW)

    def tile(place, s, slots, masked, half=None):
        count = NH * rows if half is None else rows
        first = 0 if half is None else pl.multiple_of((h if half == 0 else 1 - h) * rows, rows)
        here = pl.ds(first, count)
        query = jnp.concatenate(
            [qbuf[place, part_rows(s), g * HD : (g + 1) * HD] for g in range(heads)], axis=0
        )
        scores = []
        for slot in slots:
            scores.append(
                lax.dot_general(
                    query, kvbuf[slot, here, 0:HD],
                    (((1,), (1,)), ((), ())), preferred_element_type=jnp.float32,
                )
            )
        if masked:
            key_pos = lax.broadcasted_iota(jnp.int32, scores[0].shape, 1)
            row_pos = lax.broadcasted_iota(jnp.int32, scores[0].shape, 0) % some_rows
            seen = key_pos <= row_pos + (h * rows + s * some_rows)
            scores = [jnp.where(seen, v, LOW) for v in scores]
        old = mbuf[place, s]
        new = old
        for v in scores:
            new = jnp.maximum(new, jnp.max(v, axis=1, keepdims=True))
        factor = jnp.exp2(old - new)
        wide = jnp.concatenate([new] * (count // HD), axis=1)
        total = acc[place, s] * jnp.concatenate([factor] * 2, axis=1)
        for slot, v in zip(slots, scores):
            vals = jnp.concatenate(
                [kvbuf[slot, here, HD : 2 * HD], jnp.ones((count, HD), jnp.bfloat16)], axis=1
            )
            total += jnp.dot(
                jnp.exp2(v - wide).astype(jnp.bfloat16), vals, preferred_element_type=jnp.float32
            )
        mbuf[place, s] = new
        acc[place, s] = total

    def attend(s, step):
        lower, upper = (z + NZ - step) % NZ, (z + step) % NZ
        both = (z + step >= NZ) & (step < NZ // 2)

        @pl.when(both)
        def _():
            for place in range(NX):
                tile(place, s, (lower, upper), False)

        @pl.when(jnp.logical_not(both) & (z >= step))
        def _():
            for place in range(NX):
                tile(place, s, (lower,), False)

    pass_on(0, 1)
    for u in range(NU):
        kv_h(u).wait_recv()
        for direction in range(2):
            kv_z(direction, 1, 1, u).start()
    w_h(0, 0).start()

    @pl.loop(0, NS)
    def _(s):
        for i in range(NX - 1):
            q_x(s, i).wait_recv()
        for own in range(NX):

            @pl.when(x == own)
            def _():
                for place in range(own, NX):
                    tile(place, s, (z,), place == own)

        pl.when(s == 0)(lambda: w_step(1))
        pl.when(s == 1)(lambda: pass_on(0, 2))
        pl.when(s == 2)(lambda: pass_on(1, 1))

    @pl.loop(1, 4)
    def _(step):
        @pl.loop(0, NS)
        def _(s):
            attend(s, step)
            @pl.when((step == 3) & (z >= 4))
            def _():
                for place in range(NX):
                    tile(place, s, ((z + NZ - 4) % NZ,), False, 0)

            pl.when((s == 0) & (step < 3))(lambda: pass_on(0, step + 2))
            pl.when(s == 1)(lambda: w_step(step + 1))
            pl.when(s == 2)(lambda: pass_on(1, step + 1))

    def finish(place, s):
        total = acc[place, s, :, HD : 2 * HD]
        some = total > 0.0
        safe = jnp.where(some, total, 1.0)
        osend[s, place] = (acc[place, s, :, 0:HD] / safe).astype(jnp.bfloat16)
        lse = jnp.where(some, mbuf[place, s] + jnp.log2(safe), LOW)
        lsend[s, place] = lse.T[0:8]

    def l_x(s, d):
        place = (x + 1 + d) % NX
        return copy(L_X(s, d), lsend.at[s, place], lrecv.at[s, x], xs[d])

    def o_x(s, d):
        place = (x + 1 + d) % NX
        return copy(O_X(s, d), osend.at[s, place], orecv.at[s, x], xs[d])

    def send_shares(s):
        for d in (0, 2, 1):
            finish((x + 1 + d) % NX, s)
            l_x(s, d).start()
            o_x(s, d).start()
        finish(x, s)
        orecv[s, x] = osend[s, x]
        lrecv[s, x] = lsend[s, x]

    def a_x(s, i):
        ref = att.at[c, s, x]
        return copy(A_X(s, i), ref, ref, xs[i])

    def a_c(s, n):
        ref = att.at[c, s, (x + NX - n) % NX]
        return copy(A_C(s, n), ref, ref, other_c)

    def combine(s):
        for d in range(NX - 1):
            l_x(s, d).wait_recv()
            o_x(s, d).wait_recv()
        lses = [lrecv[s, i] for i in range(NX)]
        top = functools.reduce(jnp.maximum, lses)
        shares = [jnp.exp2(v - top) for v in lses]
        whole = sum(shares)
        shares = [v / whole for v in shares]
        shares.append(jnp.zeros((HD - 8 * NX, heads * some_rows), jnp.float32))
        turned = jnp.concatenate(shares, axis=0).T
        total = jnp.zeros((heads * some_rows, HD), jnp.float32)
        for i in range(NX):
            total += turned[:, 8 * i : 8 * i + 1] * orecv[s, i].astype(jnp.float32)
        total = total.astype(jnp.bfloat16)
        for g in range(heads):
            att[c, s, x, :, g * HD : (g + 1) * HD] = total[g * some_rows : (g + 1) * some_rows]
        for i in (0, 2, 1):
            a_x(s, i).start()
        a_c(s, 0).start()

    def gather(s):
        for i in (0, 2, 1):
            a_x(s, i).wait_recv()
            a_c(s, i + 1).start()

    def y_right(s, slot, peer):
        return copy(Y_R(s, slot), ysend_r.at[s, slot], yleft.at[s, slot], peer)

    def y_left(s, slot, peer):
        return copy(Y_L(s, slot), ysend_l.at[s, slot], yright.at[s, slot], peer)

    def put_right(s, slot, value, peer):
        ysend_r[s, slot] = value.astype(jnp.bfloat16)
        y_right(s, slot, peer).start()

    def put_left(s, slot, value, peer):
        ysend_l[s, slot] = value.astype(jnp.bfloat16)
        y_left(s, slot, peer).start()

    def project(s):
        for n in range(NX):
            a_c(s, n).wait_recv()
        mixed = [att[col, s].reshape(NX * some_rows, heads * HD) for col in range(NC)]

        total = jnp.zeros((NY * fw, NX * some_rows), jnp.float32)
        for col in range(NC):
            total += lax.dot_general(
                wbuf[col, c].reshape(NY * fw, heads * HD), mixed[col],
                (((1,), (1,)), ((), ())), preferred_element_type=jnp.float32,
            )
        part[s] = total.reshape(NY, fw, NX * some_rows)

        @pl.when(y == 0)
        def _():
            for dest in (3, 2, 1):
                put_right(s, dest, part[s, dest], right)

        @pl.when(y == 1)
        def _():
            put_left(s, 3, part[s, 0], left)

        @pl.when(y == 2)
        def _():
            put_right(s, 0, part[s, 3], right)

        @pl.when(y == 3)
        def _():
            for dest in (0, 1, 2):
                put_left(s, dest, part[s, dest], left)

    def sum_on(s):
        @pl.when(y == 1)
        def _():
            for dest, peer in ((3, across), (2, right)):
                y_right(s, dest, peer).wait_recv()
                put_right(s, dest, part[s, dest] + yleft[s, dest].astype(jnp.float32), peer)

        @pl.when(y == 2)
        def _():
            for dest, peer in ((0, across), (1, left)):
                y_left(s, dest, peer).wait_recv()
                put_left(s, dest, part[s, dest] + yright[s, dest].astype(jnp.float32), peer)

    def sum_up(s):
        @pl.when(y == 0)
        def _():
            y_left(s, 3, left).wait_recv()
            y_left(s, 0, across).wait_recv()
            fsum[s] = (
                part[s, 0] + yright[s, 3].astype(jnp.float32) + yright[s, 0].astype(jnp.float32)
            )

        @pl.when(y == 3)
        def _():
            y_right(s, 0, right).wait_recv()
            y_right(s, 3, across).wait_recv()
            fsum[s] = (
                part[s, 3] + yleft[s, 0].astype(jnp.float32) + yleft[s, 3].astype(jnp.float32)
            )

        for middle in (1, 2):

            @pl.when(y == middle)
            def _():
                y_right(s, middle, right).wait_recv()
                y_left(s, middle, left).wait_recv()
                fsum[s] = (
                    part[s, middle]
                    + yleft[s, middle].astype(jnp.float32)
                    + yright[s, middle].astype(jnp.float32)
                )

    def f_x(pair, d):
        place = (x + 1 + d) % NX
        return copy(F_X(pair, d), fsend.at[pair, place], frecv.at[pair, x], xs[d])

    def deliver(pair):
        first, second = fsum[2 * pair], fsum[2 * pair + 1]
        for place in range(NX):
            cols = slice(place * some_rows, (place + 1) * some_rows)
            both = jnp.concatenate([first[:, cols], second[:, cols]], axis=1)
            fsend[pair, place] = both.astype(jnp.bfloat16)
        for d in (0, 2, 1):
            f_x(pair, d).start()
        frecv[pair, x] = fsend[pair, x]

    def store(pair):
        for d in range(NX - 1):
            f_x(pair, d).wait_recv()
        tokens = slice(pair * 2 * some_rows, (pair + 1) * 2 * some_rows)
        out_ref[:, tokens] = frecv[pair].reshape(NX * fw, 2 * some_rows)

    def stage(turn, late, action, count=NS):
        pl.when((turn >= late) & (turn < late + count))(lambda: action(turn - late))

    @pl.loop(0, NS + 4)
    def _(turn):
        @pl.when(turn < NS)
        def _():
            @pl.when(z >= 4)
            def _():
                for place in range(NX):
                    tile(place, turn, ((z + NZ - 4) % NZ,), False, 1)

            send_shares(turn)

        stage(turn, 1, combine)

        @pl.when(turn == 1)
        def _():
            for direction in range(2):
                for step in range(5 - direction):
                    if step > 0 or direction == 0:
                        w_h(direction, step).wait_recv()
            for i in range(NZ // 2):
                w_c(i).start()

        stage(turn, 2, gather)

        @pl.when(turn == 2)
        def _():
            for i in range(NZ // 2):
                w_c(i).wait_recv()

        stage(turn, 2, project)

        stage(turn, 3, sum_on)

        stage(turn, 4, sum_up)

        @pl.when((turn == 5) | (turn == 7))
        def _():
            deliver((turn - 5) // 2)

    for pair in range(NS // 2):
        store(pair)

    for u in range(NU):
        kv_h(u).wait_send()
        for direction in range(2):
            for half in range(2):
                for step in range(1, 5):
                    if step < 4 or direction == half:
                        kv_z(direction, half, step, u).wait_send()
    for direction in range(2):
        for step in range(1, 5 - direction):
            w_z(direction, step).wait_send()
        for step in range(direction, 5 - direction):
            w_h(direction, step).wait_send()
    for i in range(NZ // 2):
        w_c(i).wait_send()
    for pair in range(NS // 2):
        for d in range(NX - 1):
            f_x(pair, d).wait_send()

    @pl.loop(0, NS)
    def _(s):
        for d in range(NX - 1):
            q_x(s, d).wait_send()
            l_x(s, d).wait_send()
            o_x(s, d).wait_send()
            a_x(s, d).wait_send()
        for n in range(NX):
            a_c(s, n).wait_send()

        @pl.when(y == 0)
        def _():
            for dest in (3, 2, 1):
                y_right(s, dest, right).wait_send()

        @pl.when(y == 1)
        def _():
            y_left(s, 3, left).wait_send()
            y_right(s, 3, across).wait_send()
            y_right(s, 2, right).wait_send()

        @pl.when(y == 2)
        def _():
            y_right(s, 0, right).wait_send()
            y_left(s, 0, across).wait_send()
            y_left(s, 1, left).wait_send()

        @pl.when(y == 3)
        def _():
            for dest in (0, 1, 2):
                y_left(s, dest, left).wait_send()


def body(queries, keys, values, out_weight):
    rows = queries.shape[0]
    wrows = out_weight.shape[0]
    cols = queries.shape[1]
    heads = cols // HD
    fw = NH * wrows
    some = rows // NS
    positions = lax.axis_index("ctx") * rows + jnp.arange(rows, dtype=jnp.int32)
    cosine, sines = rotation(positions)
    vmem = pl.BlockSpec(memory_space=pltpu.VMEM)
    bf16, f32 = jnp.bfloat16, jnp.float32
    turned = pl.pallas_call(
        kernel,
        out_shape=jax.ShapeDtypeStruct((NX * fw, rows), bf16),
        in_specs=[vmem] * 6,
        out_specs=vmem,
        scratch_shapes=[
            pltpu.VMEM((NX, rows, cols), bf16),
            pltpu.VMEM((NZ, NH * rows, 2 * HD), bf16),
            pltpu.VMEM((NC, 2, NZ // 2, fw, cols), bf16),
            pltpu.VMEM((NX, NS, heads * some, 2 * HD), f32),
            pltpu.VMEM((NX, NS, heads * some, HD), f32),
            pltpu.VMEM((NS, NX, heads * some, HD), bf16),
            pltpu.VMEM((NS, NX, heads * some, HD), bf16),
            pltpu.VMEM((NS, NX, 8, heads * some), f32),
            pltpu.VMEM((NS, NX, 8, heads * some), f32),
            pltpu.VMEM((NC, NS, NX, some, cols), bf16),
            pltpu.VMEM((NS, NY, fw, NX * some), f32),
            pltpu.VMEM((NS, NY, fw, NX * some), bf16),
            pltpu.VMEM((NS, NY, fw, NX * some), bf16),
            pltpu.VMEM((NS, NY, fw, NX * some), bf16),
            pltpu.VMEM((NS, NY, fw, NX * some), bf16),
            pltpu.VMEM((NS, fw, NX * some), f32),
            pltpu.VMEM((NS // 2, NX, fw, 2 * some), bf16),
            pltpu.VMEM((NS // 2, NX, fw, 2 * some), bf16),
            pltpu.SemaphoreType.DMA((COUNT,)),
            pltpu.SemaphoreType.DMA((COUNT,)),
        ],
        compiler_params=pltpu.CompilerParams(
            collective_id=0, has_side_effects=True, vmem_limit_bytes=56 * 2**20
        ),
        name="attention_layer",
    )(queries, keys, values, out_weight, cosine, sines)
    return turned.T


def solution(mesh):
    placed = (P("ctx", "tp"), P("ctx", "tp"), P("ctx", "tp"), P("ctx", "tp"))
    return jax.shard_map(
        body, mesh=mesh, in_specs=placed, out_specs=P("ctx", "tp"), check_vma=False
    )
```

```python
import functools
import math

import jax
import jax.numpy as jnp
from jax import lax
from jax.experimental import pallas as pl
from jax.experimental.pallas import tpu as pltpu
from jax.sharding import PartitionSpec as P

HD = 128
NZ, NX, NH, NY, NC = 8, 4, 2, 4, 2
NS = 4
NU = 2
MESH = pl.DeviceIdType.MESH
LOW = -1e30


def rotation(positions):
    half_width = HD // 2
    frequency = jnp.exp(
        -(jnp.arange(half_width, dtype=jnp.float32) / half_width) * math.log(1000000.0)
    )
    angles = positions.astype(jnp.float32)[:, None] * frequency[None, :]
    cosine = jnp.cos(angles)
    sines = jnp.sin(angles)
    return cosine, sines


COUNT = 0


def numbers(*shape):
    global COUNT
    total = math.prod(shape)
    first = COUNT
    COUNT += total
    strides = [math.prod(shape[i + 1 :]) for i in range(len(shape))]
    return lambda *index: first + sum(i * s for i, s in zip(index, strides))


KV_H = numbers(NU)
W_H = numbers(2, 5)
Q_X = numbers(NS, 3)
KV_Z = numbers(2, 2, 4, NU)
W_Z = numbers(2, 4)
W_C = numbers(4)
O_X = numbers(NS, 3)
L_X = numbers(NS, 3)
A_X = numbers(NS, 3)
A_C = numbers(NS, 4)
Y_R = numbers(NS, 4)
Y_L = numbers(NS, 4)
F_X = numbers(NS // 2, 3)


def kernel(
    q_ref, k_ref, v_ref, w_ref, cos_ref, sin_ref, out_ref,
    qbuf, kvbuf, wbuf, acc, mbuf, osend, orecv, lsend, lrecv, att, part,
    yleft, yright, ysend_r, ysend_l, fsum, fsend, frecv, ssem, rsem,
):
    rows = q_ref.shape[0]
    wrows = w_ref.shape[0]
    heads = q_ref.shape[1] // HD
    fw = NH * wrows
    some_rows = rows // NS
    ctx = lax.axis_index("ctx")
    tp = lax.axis_index("tp")
    z, x, h = ctx // (NX * NH), (ctx // NH) % NX, ctx % NH
    y, c = tp // NC, tp % NC

    def at(z=z, x=x, h=h, y=y, c=c):
        return (z * (NX * NH) + x * NH + h, y * NC + c)

    up, down = at(z=(z + 1) % NZ), at(z=(z + NZ - 1) % NZ)
    xs = [at(x=(x + d) % NX) for d in range(1, NX)]
    other_h, other_c = at(h=1 - h), at(c=1 - c)
    ring = h * NY + y
    y_next = (ring + 1) % (NH * NY)
    y_prev = (ring + NH * NY - 1) % (NH * NY)
    right = at(h=y_next // NY, y=y_next % NY)
    left = at(h=y_prev // NY, y=y_prev % NY)

    across = at(y=(y + 2) % NY)

    barrier = pltpu.get_barrier_semaphore()
    peers = [other_h, up, down, *xs, across, right, left, other_c]
    for peer in peers:
        pl.semaphore_signal(barrier, 1, device_id=peer, device_id_type=MESH)

    def copy(number, src, dst, peer):
        return pltpu.make_async_remote_copy(
            src_ref=src, dst_ref=dst, send_sem=ssem.at[number], recv_sem=rsem.at[number],
            device_id=peer, device_id_type=MESH,
        )

    def own_rows(n):
        return pl.ds(pl.multiple_of(h * n, 16), n)

    cosine = jnp.concatenate([cos_ref[...], cos_ref[...]], axis=1)
    sines = jnp.concatenate([-sin_ref[...], sin_ref[...]], axis=1)

    def rotated(source):
        wide = source.astype(jnp.float32)
        return wide * cosine + pltpu.roll(wide, HD // 2, 1) * sines

    def slot_of(direction, step):
        return (z + NZ - (step - 1)) % NZ if direction == 0 else (z + step - 1) % NZ

    piece = rows // NU

    def kv_rows(half, u):
        first = h * rows if half == 0 else (1 - h) * rows
        return pl.ds(pl.multiple_of(first + u * piece, piece), piece)

    def kv_h(u):
        ref = kvbuf.at[z, kv_rows(0, u)]
        return copy(KV_H(u), ref, ref, other_h)

    def kv_z(direction, half, step, u):
        ref = kvbuf.at[slot_of(direction, step), kv_rows(half, u)]
        return copy(KV_Z(direction, half, step - 1, u), ref, ref, (up, down)[direction])

    def w_at(slot):
        return wbuf.at[c, slot % 2, slot // 2, own_rows(wrows)]

    def w_z(direction, step):
        ref = w_at(slot_of(direction, step))
        return copy(W_Z(direction, step - 1), ref, ref, (up, down)[direction])

    def w_h(direction, step):
        ref = w_at(slot_of(direction, step + 1))
        return copy(W_H(direction, step), ref, ref, other_h)

    def w_c(i):
        ref = wbuf.at[c, 1 - c, i]
        return copy(W_C(i), ref, ref, other_c)

    def part_rows(s):
        return pl.ds(pl.multiple_of(s * some_rows, some_rows), some_rows)

    def q_x(s, i):
        ref = qbuf.at[x, part_rows(s)]
        return copy(Q_X(s, i), ref, ref, xs[i])

    def when(condition, action):
        if condition is True:
            action()
        elif condition is not False:
            pl.when(condition)(action)

    def pass_on(half, step):
        last = 4 if half == 0 else 3
        for u in range(NU):
            for direction in range(2):
                steps = last if direction == 0 else 7 - last
                here = functools.partial(kv_z, direction, half, step, u)
                there = functools.partial(kv_z, direction, half, step + 1, u)
                when(step <= steps, lambda: here().wait_recv())
                when(step < steps, lambda: there().start())

    def w_step(step):
        for direction in range(2):
            steps = 4 - direction
            when(step <= steps, lambda: w_z(direction, step).wait_recv())
            when(step < steps, lambda: w_z(direction, step + 1).start())
            when(step <= steps, lambda: w_h(direction, step).start())

    kvbuf[z, own_rows(rows), 0:HD] = rotated(k_ref[...]).astype(jnp.bfloat16)
    kvbuf[z, own_rows(rows), HD : 2 * HD] = v_ref[...]
    scale = math.log2(math.e) / math.sqrt(HD)
    for g in range(heads):
        cols = slice(g * HD, (g + 1) * HD)
        qbuf[x, :, cols] = (rotated(q_ref[:, cols]) * scale).astype(jnp.bfloat16)
    wbuf[c, z % 2, z // 2, own_rows(wrows)] = w_ref[...]
    pl.semaphore_wait(barrier, len(peers))

    for u in range(NU):
        kv_h(u).start()
    for u in range(NU):
        for direction in range(2):
            kv_z(direction, 0, 1, u).start()

    w_z(0, 1).start()
    w_z(1, 1).start()

    @pl.loop(0, NS)
    def _(s):
        for i in (0, 2, 1):
            q_x(s, i).start()

    acc[...] = jnp.zeros_like(acc)
    mbuf[...] = jnp.full_like(mbuf, LOW)

    def tile(place, s, slots, masked, half=None):
        count = NH * rows if half is None else rows
        first = 0 if half is None else pl.multiple_of((h if half == 0 else 1 - h) * rows, rows)
        here = pl.ds(first, count)
        query = jnp.concatenate(
            [qbuf[place, part_rows(s), g * HD : (g + 1) * HD] for g in range(heads)], axis=0
        )
        scores = []
        for slot in slots:
            scores.append(
                lax.dot_general(
                    query, kvbuf[slot, here, 0:HD],
                    (((1,), (1,)), ((), ())), preferred_element_type=jnp.float32,
                )
            )
        if masked:
            key_pos = lax.broadcasted_iota(jnp.int32, scores[0].shape, 1)
            row_pos = lax.broadcasted_iota(jnp.int32, scores[0].shape, 0) % some_rows
            seen = key_pos <= row_pos + (h * rows + s * some_rows)
            scores = [jnp.where(seen, v, LOW) for v in scores]
        old = mbuf[place, s]
        new = old
        for v in scores:
            new = jnp.maximum(new, jnp.max(v, axis=1, keepdims=True))
        factor = jnp.exp2(old - new)
        wide = jnp.concatenate([new] * (count // HD), axis=1)
        total = acc[place, s] * jnp.concatenate([factor] * 2, axis=1)
        for slot, v in zip(slots, scores):
            vals = jnp.concatenate(
                [kvbuf[slot, here, HD : 2 * HD], jnp.ones((count, HD), jnp.bfloat16)], axis=1
            )
            total += jnp.dot(
                jnp.exp2(v - wide).astype(jnp.bfloat16), vals, preferred_element_type=jnp.float32
            )
        mbuf[place, s] = new
        acc[place, s] = total

    def attend(pair, step):
        lower, upper = (z + NZ - step) % NZ, (z + step) % NZ
        both = (z + step >= NZ) & (step < NZ // 2)

        @pl.when(both)
        def _():
            for place in range(NX):
                for s in range(2):
                    tile(place, 2 * pair + s, (lower, upper), False)

        @pl.when(jnp.logical_not(both) & (z >= step))
        def _():
            for place in range(NX):
                for s in range(2):
                    tile(place, 2 * pair + s, (lower,), False)

    pass_on(0, 1)
    for u in range(NU):
        kv_h(u).wait_recv()
        for direction in range(2):
            kv_z(direction, 1, 1, u).start()
    w_h(0, 0).start()

    @pl.loop(0, NS)
    def _(s):
        for i in range(NX - 1):
            q_x(s, i).wait_recv()
        for own in range(NX):

            @pl.when(x == own)
            def _():
                for place in range(own, NX):
                    tile(place, s, (z,), place == own)

        pl.when(s == 0)(lambda: w_step(1))
        pl.when(s == 2)(lambda: pass_on(0, 2))
        pl.when(s == 3)(lambda: pass_on(1, 1))

    @pl.loop(1, 4)
    def _(step):
        @pl.loop(0, NS // 2)
        def _(pair):
            attend(pair, step)

            @pl.when((step == 3) & (z >= 4))
            def _():
                for place in range(NX):
                    for s in range(2):
                        tile(place, 2 * pair + s, ((z + NZ - 4) % NZ,), False, 0)

            pl.when((pair == 0) & (step < 3))(lambda: pass_on(0, step + 2))
            pl.when(pair == 0)(lambda: w_step(step + 1))
            pl.when(pair == 1)(lambda: pass_on(1, step + 1))

    def finish(place, s):
        total = acc[place, s, :, HD : 2 * HD]
        some = total > 0.0
        safe = jnp.where(some, total, 1.0)
        osend[s, place] = (acc[place, s, :, 0:HD] / safe).astype(jnp.bfloat16)
        lse = jnp.where(some, mbuf[place, s] + jnp.log2(safe), LOW)
        lsend[s, place] = lse.T[0:8]

    def l_x(s, d):
        place = (x + 1 + d) % NX
        return copy(L_X(s, d), lsend.at[s, place], lrecv.at[s, x], xs[d])

    def o_x(s, d):
        place = (x + 1 + d) % NX
        return copy(O_X(s, d), osend.at[s, place], orecv.at[s, x], xs[d])

    def send_shares(s):
        for d in (1, 0, 2):
            finish((x + 1 + d) % NX, s)
            l_x(s, d).start()
            o_x(s, d).start()
        finish(x, s)
        orecv[s, x] = osend[s, x]
        lrecv[s, x] = lsend[s, x]

    def a_x(s, i):
        ref = att.at[c, s, x]
        return copy(A_X(s, i), ref, ref, xs[i])

    def a_c(s, n):
        ref = att.at[c, s, (x + NX - n) % NX]
        return copy(A_C(s, n), ref, ref, other_c)

    def combine(s):
        for d in range(NX - 1):
            l_x(s, d).wait_recv()
            o_x(s, d).wait_recv()
        lses = [lrecv[s, i] for i in range(NX)]
        top = functools.reduce(jnp.maximum, lses)
        shares = [jnp.exp2(v - top) for v in lses]
        whole = sum(shares)
        shares = [v / whole for v in shares]
        shares.append(jnp.zeros((HD - 8 * NX, heads * some_rows), jnp.float32))
        turned = jnp.concatenate(shares, axis=0).T
        total = jnp.zeros((heads * some_rows, HD), jnp.float32)
        for i in range(NX):
            total += turned[:, 8 * i : 8 * i + 1] * orecv[s, i].astype(jnp.float32)
        total = total.astype(jnp.bfloat16)
        for g in range(heads):
            att[c, s, x, :, g * HD : (g + 1) * HD] = total[g * some_rows : (g + 1) * some_rows]
        for i in (1, 0, 2):
            a_x(s, i).start()
        a_c(s, 0).start()

    def gather(s):
        for i in (0, 2, 1):
            a_x(s, i).wait_recv()
            a_c(s, i + 1).start()

    def y_right(s, slot, peer):
        return copy(Y_R(s, slot), ysend_r.at[s, slot], yleft.at[s, slot], peer)

    def y_left(s, slot, peer):
        return copy(Y_L(s, slot), ysend_l.at[s, slot], yright.at[s, slot], peer)

    def put_right(s, slot, value, peer):
        ysend_r[s, slot] = value.astype(jnp.bfloat16)
        y_right(s, slot, peer).start()

    def put_left(s, slot, value, peer):
        ysend_l[s, slot] = value.astype(jnp.bfloat16)
        y_left(s, slot, peer).start()

    def project(s):
        for n in range(NX):
            a_c(s, n).wait_recv()
        mixed = [att[col, s].reshape(NX * some_rows, heads * HD) for col in range(NC)]

        total = jnp.zeros((NY * fw, NX * some_rows), jnp.float32)
        for col in range(NC):
            total += lax.dot_general(
                wbuf[col, c].reshape(NY * fw, heads * HD), mixed[col],
                (((1,), (1,)), ((), ())), preferred_element_type=jnp.float32,
            )
        part[s] = total.reshape(NY, fw, NX * some_rows)

        @pl.when(y == 0)
        def _():
            for dest in (3, 2, 1):
                put_right(s, dest, part[s, dest], right)

        @pl.when(y == 1)
        def _():
            put_left(s, 3, part[s, 0], left)

        @pl.when(y == 2)
        def _():
            put_right(s, 0, part[s, 3], right)

        @pl.when(y == 3)
        def _():
            for dest in (0, 1, 2):
                put_left(s, dest, part[s, dest], left)

    def sum_on(s):
        @pl.when(y == 1)
        def _():
            for dest, peer in ((3, across), (2, right)):
                y_right(s, dest, peer).wait_recv()
                put_right(s, dest, part[s, dest] + yleft[s, dest].astype(jnp.float32), peer)

        @pl.when(y == 2)
        def _():
            for dest, peer in ((0, across), (1, left)):
                y_left(s, dest, peer).wait_recv()
                put_left(s, dest, part[s, dest] + yright[s, dest].astype(jnp.float32), peer)

    def sum_up(s):
        @pl.when(y == 0)
        def _():
            y_left(s, 3, left).wait_recv()
            y_left(s, 0, across).wait_recv()
            fsum[s] = (
                part[s, 0] + yright[s, 3].astype(jnp.float32) + yright[s, 0].astype(jnp.float32)
            )

        @pl.when(y == 3)
        def _():
            y_right(s, 0, right).wait_recv()
            y_right(s, 3, across).wait_recv()
            fsum[s] = (
                part[s, 3] + yleft[s, 0].astype(jnp.float32) + yleft[s, 3].astype(jnp.float32)
            )

        for middle in (1, 2):

            @pl.when(y == middle)
            def _():
                y_right(s, middle, right).wait_recv()
                y_left(s, middle, left).wait_recv()
                fsum[s] = (
                    part[s, middle]
                    + yleft[s, middle].astype(jnp.float32)
                    + yright[s, middle].astype(jnp.float32)
                )

    def f_x(pair, d):
        place = (x + 1 + d) % NX
        return copy(F_X(pair, d), fsend.at[pair, place], frecv.at[pair, x], xs[d])

    def deliver(pair):
        first, second = fsum[2 * pair], fsum[2 * pair + 1]
        for place in range(NX):
            cols = slice(place * some_rows, (place + 1) * some_rows)
            both = jnp.concatenate([first[:, cols], second[:, cols]], axis=1)
            fsend[pair, place] = both.astype(jnp.bfloat16)
        for d in (0, 2, 1):
            f_x(pair, d).start()
        frecv[pair, x] = fsend[pair, x]

    def store(pair):
        for d in range(NX - 1):
            f_x(pair, d).wait_recv()
        tokens = slice(pair * 2 * some_rows, (pair + 1) * 2 * some_rows)
        out_ref[:, tokens] = frecv[pair].reshape(NX * fw, 2 * some_rows)

    def stage(turn, late, action, count=NS):
        pl.when((turn >= late) & (turn < late + count))(lambda: action(turn - late))

    @pl.loop(0, NS + 4)
    def _(turn):
        @pl.when(turn < NS)
        def _():
            @pl.when(z >= 4)
            def _():
                for place in range(NX):
                    tile(place, turn, ((z + NZ - 4) % NZ,), False, 1)

            send_shares(turn)

        stage(turn, 1, combine)

        @pl.when(turn == 2)
        def _():
            for direction in range(2):
                for step in range(5 - direction):
                    if step > 0 or direction == 0:
                        w_h(direction, step).wait_recv()
            for i in range(NZ // 2):
                w_c(i).start()

        stage(turn, 2, gather)

        @pl.when(turn == 2)
        def _():
            for i in range(NZ // 2):
                w_c(i).wait_recv()

        stage(turn, 2, project)

        stage(turn, 3, sum_on)

        stage(turn, 4, sum_up)

        @pl.when((turn == 5) | (turn == 7))
        def _():
            deliver((turn - 5) // 2)

    for pair in range(NS // 2):
        store(pair)

    for u in range(NU):
        kv_h(u).wait_send()
        for direction in range(2):
            for half in range(2):
                for step in range(1, 5):
                    if step < 4 or direction == half:
                        kv_z(direction, half, step, u).wait_send()
    for direction in range(2):
        for step in range(1, 5 - direction):
            w_z(direction, step).wait_send()
        for step in range(direction, 5 - direction):
            w_h(direction, step).wait_send()
    for i in range(NZ // 2):
        w_c(i).wait_send()
    for pair in range(NS // 2):
        for d in range(NX - 1):
            f_x(pair, d).wait_send()

    @pl.loop(0, NS)
    def _(s):
        for d in range(NX - 1):
            q_x(s, d).wait_send()
            l_x(s, d).wait_send()
            o_x(s, d).wait_send()
            a_x(s, d).wait_send()
        for n in range(NX):
            a_c(s, n).wait_send()

        @pl.when(y == 0)
        def _():
            for dest in (3, 2, 1):
                y_right(s, dest, right).wait_send()

        @pl.when(y == 1)
        def _():
            y_left(s, 3, left).wait_send()
            y_right(s, 3, across).wait_send()
            y_right(s, 2, right).wait_send()

        @pl.when(y == 2)
        def _():
            y_right(s, 0, right).wait_send()
            y_left(s, 0, across).wait_send()
            y_left(s, 1, left).wait_send()

        @pl.when(y == 3)
        def _():
            for dest in (0, 1, 2):
                y_left(s, dest, left).wait_send()


def body(queries, keys, values, out_weight):
    rows = queries.shape[0]
    wrows = out_weight.shape[0]
    cols = queries.shape[1]
    heads = cols // HD
    fw = NH * wrows
    some = rows // NS
    positions = lax.axis_index("ctx") * rows + jnp.arange(rows, dtype=jnp.int32)
    cosine, sines = rotation(positions)
    vmem = pl.BlockSpec(memory_space=pltpu.VMEM)
    bf16, f32 = jnp.bfloat16, jnp.float32
    turned = pl.pallas_call(
        kernel,
        out_shape=jax.ShapeDtypeStruct((NX * fw, rows), bf16),
        in_specs=[vmem] * 6,
        out_specs=vmem,
        scratch_shapes=[
            pltpu.VMEM((NX, rows, cols), bf16),
            pltpu.VMEM((NZ, NH * rows, 2 * HD), bf16),
            pltpu.VMEM((NC, 2, NZ // 2, fw, cols), bf16),
            pltpu.VMEM((NX, NS, heads * some, 2 * HD), f32),
            pltpu.VMEM((NX, NS, heads * some, HD), f32),
            pltpu.VMEM((NS, NX, heads * some, HD), bf16),
            pltpu.VMEM((NS, NX, heads * some, HD), bf16),
            pltpu.VMEM((NS, NX, 8, heads * some), f32),
            pltpu.VMEM((NS, NX, 8, heads * some), f32),
            pltpu.VMEM((NC, NS, NX, some, cols), bf16),
            pltpu.VMEM((NS, NY, fw, NX * some), f32),
            pltpu.VMEM((NS, NY, fw, NX * some), bf16),
            pltpu.VMEM((NS, NY, fw, NX * some), bf16),
            pltpu.VMEM((NS, NY, fw, NX * some), bf16),
            pltpu.VMEM((NS, NY, fw, NX * some), bf16),
            pltpu.VMEM((NS, fw, NX * some), f32),
            pltpu.VMEM((NS // 2, NX, fw, 2 * some), bf16),
            pltpu.VMEM((NS // 2, NX, fw, 2 * some), bf16),
            pltpu.SemaphoreType.DMA((COUNT,)),
            pltpu.SemaphoreType.DMA((COUNT,)),
        ],
        compiler_params=pltpu.CompilerParams(
            collective_id=0, has_side_effects=True, vmem_limit_bytes=56 * 2**20
        ),
        name="attention_layer",
    )(queries, keys, values, out_weight, cosine, sines)
    return turned.T


def solution(mesh):
    placed = (P("ctx", "tp"), P("ctx", "tp"), P("ctx", "tp"), P("ctx", "tp"))
    return jax.shard_map(
        body, mesh=mesh, in_specs=placed, out_specs=P("ctx", "tp"), check_vma=False
    )
```

```python
import functools
import math

import jax
import jax.numpy as jnp
from jax import lax
from jax.experimental import pallas as pl
from jax.experimental.pallas import tpu as pltpu
from jax.sharding import PartitionSpec as P

HD = 128
NZ, NX, NH, NY, NC = 8, 4, 2, 4, 2
NS = 4
NU = 2
MESH = pl.DeviceIdType.MESH
LOW = -1e30


def rotation(positions):
    half_width = HD // 2
    frequency = jnp.exp(
        -(jnp.arange(half_width, dtype=jnp.float32) / half_width) * math.log(1000000.0)
    )
    angles = positions.astype(jnp.float32)[:, None] * frequency[None, :]
    cosine = jnp.cos(angles)
    sines = jnp.sin(angles)
    return cosine, sines


COUNT = 0


def numbers(*shape):
    global COUNT
    total = math.prod(shape)
    first = COUNT
    COUNT += total
    strides = [math.prod(shape[i + 1 :]) for i in range(len(shape))]
    return lambda *index: first + sum(i * s for i, s in zip(index, strides))


KV_H = numbers(NU)
W_H = numbers(2, 5)
Q_X = numbers(NS, 3)
KV_Z = numbers(2, 2, 4, NU)
W_Z = numbers(2, 4)
W_C = numbers(4)
O_X = numbers(NS, 3)
L_X = numbers(NS, 3)
A_X = numbers(NS, 3)
A_C = numbers(NS, 4)
Y_R = numbers(NS, 4)
Y_L = numbers(NS, 4)
F_X = numbers(NS // 2, 3)


def kernel(
    q_ref, k_ref, v_ref, w_ref, cos_ref, sin_ref, out_ref,
    qbuf, kvbuf, wbuf, acc, mbuf, osend, orecv, lsend, lrecv, att, part,
    yleft, yright, ysend_r, ysend_l, fsum, fsend, frecv, ssem, rsem,
):
    rows = q_ref.shape[0]
    wrows = w_ref.shape[0]
    heads = q_ref.shape[1] // HD
    fw = NH * wrows
    some_rows = rows // NS
    ctx = lax.axis_index("ctx")
    tp = lax.axis_index("tp")
    z, x, h = ctx // (NX * NH), (ctx // NH) % NX, ctx % NH
    y, c = tp // NC, tp % NC

    def at(z=z, x=x, h=h, y=y, c=c):
        return (z * (NX * NH) + x * NH + h, y * NC + c)

    up, down = at(z=(z + 1) % NZ), at(z=(z + NZ - 1) % NZ)
    xs = [at(x=(x + d) % NX) for d in range(1, NX)]
    other_h, other_c = at(h=1 - h), at(c=1 - c)
    ring = h * NY + y
    y_next = (ring + 1) % (NH * NY)
    y_prev = (ring + NH * NY - 1) % (NH * NY)
    right = at(h=y_next // NY, y=y_next % NY)
    left = at(h=y_prev // NY, y=y_prev % NY)

    across = at(y=(y + 2) % NY)

    barrier = pltpu.get_barrier_semaphore()
    peers = [other_h, up, down, *xs, across, right, left, other_c]
    for peer in peers:
        pl.semaphore_signal(barrier, 1, device_id=peer, device_id_type=MESH)

    def copy(number, src, dst, peer):
        return pltpu.make_async_remote_copy(
            src_ref=src, dst_ref=dst, send_sem=ssem.at[number], recv_sem=rsem.at[number],
            device_id=peer, device_id_type=MESH,
        )

    def own_rows(n):
        return pl.ds(pl.multiple_of(h * n, 16), n)

    cosine = jnp.concatenate([cos_ref[...], cos_ref[...]], axis=1)
    sines = jnp.concatenate([-sin_ref[...], sin_ref[...]], axis=1)

    def rotated(source):
        wide = source.astype(jnp.float32)
        return wide * cosine + pltpu.roll(wide, HD // 2, 1) * sines

    def slot_of(direction, step):
        return (z + NZ - (step - 1)) % NZ if direction == 0 else (z + step - 1) % NZ

    piece = rows // NU

    def kv_rows(half, u):
        first = h * rows if half == 0 else (1 - h) * rows
        return pl.ds(pl.multiple_of(first + u * piece, piece), piece)

    def kv_h(u):
        ref = kvbuf.at[z, kv_rows(0, u)]
        return copy(KV_H(u), ref, ref, other_h)

    def kv_z(direction, half, step, u):
        ref = kvbuf.at[slot_of(direction, step), kv_rows(half, u)]
        return copy(KV_Z(direction, half, step - 1, u), ref, ref, (up, down)[direction])

    def w_at(slot):
        return wbuf.at[c, slot % 2, slot // 2, own_rows(wrows)]

    def w_z(direction, step):
        ref = w_at(slot_of(direction, step))
        return copy(W_Z(direction, step - 1), ref, ref, (up, down)[direction])

    def w_h(direction, step):
        ref = w_at(slot_of(direction, step + 1))
        return copy(W_H(direction, step), ref, ref, other_h)

    def w_c(i):
        ref = wbuf.at[c, 1 - c, i]
        return copy(W_C(i), ref, ref, other_c)

    def part_rows(s):
        return pl.ds(pl.multiple_of(s * some_rows, some_rows), some_rows)

    def q_x(s, i):
        ref = qbuf.at[x, part_rows(s)]
        return copy(Q_X(s, i), ref, ref, xs[i])

    def when(condition, action):
        if condition is True:
            action()
        elif condition is not False:
            pl.when(condition)(action)

    def pass_on(half, step):
        last = 4 if half == 0 else 3
        for u in range(NU):
            for direction in range(2):
                steps = last if direction == 0 else 7 - last
                here = functools.partial(kv_z, direction, half, step, u)
                there = functools.partial(kv_z, direction, half, step + 1, u)
                when(step <= steps, lambda: here().wait_recv())
                when(step < steps, lambda: there().start())

    def w_step(step):
        for direction in range(2):
            steps = 4 - direction
            when(step <= steps, lambda: w_z(direction, step).wait_recv())
            when(step < steps, lambda: w_z(direction, step + 1).start())
            when(step <= steps, lambda: w_h(direction, step).start())

    kvbuf[z, own_rows(rows), 0:HD] = rotated(k_ref[...]).astype(jnp.bfloat16)
    kvbuf[z, own_rows(rows), HD : 2 * HD] = v_ref[...]
    scale = math.log2(math.e) / math.sqrt(HD)
    for g in range(heads):
        cols = slice(g * HD, (g + 1) * HD)
        qbuf[x, :, cols] = (rotated(q_ref[:, cols]) * scale).astype(jnp.bfloat16)
    wbuf[c, z % 2, z // 2, own_rows(wrows)] = w_ref[...]
    pl.semaphore_wait(barrier, len(peers))

    for u in range(NU):
        kv_h(u).start()
    for u in range(NU):
        for direction in range(2):
            kv_z(direction, 0, 1, u).start()

    w_z(0, 1).start()
    w_z(1, 1).start()

    @pl.loop(0, NS)
    def _(s):
        for i in (0, 2, 1):
            q_x(s, i).start()

    acc[...] = jnp.zeros_like(acc)
    mbuf[...] = jnp.full_like(mbuf, LOW)

    def tile(place, s, slots, masked, half=None):
        count = NH * rows if half is None else rows
        first = 0 if half is None else pl.multiple_of((h if half == 0 else 1 - h) * rows, rows)
        here = pl.ds(first, count)
        query = jnp.concatenate(
            [qbuf[place, part_rows(s), g * HD : (g + 1) * HD] for g in range(heads)], axis=0
        )
        scores = []
        for slot in slots:
            scores.append(
                lax.dot_general(
                    query, kvbuf[slot, here, 0:HD],
                    (((1,), (1,)), ((), ())), preferred_element_type=jnp.float32,
                )
            )
        if masked:
            key_pos = lax.broadcasted_iota(jnp.int32, scores[0].shape, 1)
            row_pos = lax.broadcasted_iota(jnp.int32, scores[0].shape, 0) % some_rows
            seen = key_pos <= row_pos + (h * rows + s * some_rows)
            scores = [jnp.where(seen, v, LOW) for v in scores]
        old = mbuf[place, s]
        new = old
        for v in scores:
            new = jnp.maximum(new, jnp.max(v, axis=1, keepdims=True))
        factor = jnp.exp2(old - new)
        wide = jnp.concatenate([new] * (count // HD), axis=1)
        total = acc[place, s] * jnp.concatenate([factor] * 2, axis=1)
        for slot, v in zip(slots, scores):
            vals = jnp.concatenate(
                [kvbuf[slot, here, HD : 2 * HD], jnp.ones((count, HD), jnp.bfloat16)], axis=1
            )
            total += jnp.dot(
                jnp.exp2(v - wide).astype(jnp.bfloat16), vals, preferred_element_type=jnp.float32
            )
        mbuf[place, s] = new
        acc[place, s] = total

    def attend(pair, step):
        lower, upper = (z + NZ - step) % NZ, (z + step) % NZ
        both = (z + step >= NZ) & (step < NZ // 2)

        @pl.when(both)
        def _():
            for place in range(NX):
                for s in range(2):
                    tile(place, 2 * pair + s, (lower, upper), False)

        @pl.when(jnp.logical_not(both) & (z >= step))
        def _():
            for place in range(NX):
                for s in range(2):
                    tile(place, 2 * pair + s, (lower,), False)

    pass_on(0, 1)
    for u in range(NU):
        kv_h(u).wait_recv()
        for direction in range(2):
            kv_z(direction, 1, 1, u).start()
    w_h(0, 0).start()

    @pl.loop(0, NS)
    def _(s):
        for i in range(NX - 1):
            q_x(s, i).wait_recv()
        for own in range(NX):

            @pl.when(x == own)
            def _():
                for place in range(own, NX):
                    tile(place, s, (z,), place == own)

        pl.when(s == 0)(lambda: w_step(1))
        pl.when(s == 2)(lambda: pass_on(0, 2))
        pl.when(s == 3)(lambda: pass_on(1, 1))

    @pl.loop(1, 4)
    def _(step):
        @pl.loop(0, NS // 2)
        def _(pair):
            attend(pair, step)

            @pl.when((step == 3) & (z >= 4))
            def _():
                for place in range(NX):
                    for s in range(2):
                        tile(place, 2 * pair + s, ((z + NZ - 4) % NZ,), False, 0)

            pl.when(pair == 0)(lambda: w_step(step + 1))
            pl.when((pair == 0) & (step < 3))(lambda: pass_on(0, step + 2))
            pl.when(pair == 1)(lambda: pass_on(1, step + 1))

    def finish(place, s):
        total = acc[place, s, :, HD : 2 * HD]
        some = total > 0.0
        safe = jnp.where(some, total, 1.0)
        osend[s, place] = (acc[place, s, :, 0:HD] / safe).astype(jnp.bfloat16)
        lse = jnp.where(some, mbuf[place, s] + jnp.log2(safe), LOW)
        lsend[s, place] = lse.T[0:8]

    def l_x(s, d):
        place = (x + 1 + d) % NX
        return copy(L_X(s, d), lsend.at[s, place], lrecv.at[s, x], xs[d])

    def o_x(s, d):
        place = (x + 1 + d) % NX
        return copy(O_X(s, d), osend.at[s, place], orecv.at[s, x], xs[d])

    def send_shares(s):
        for d in (1, 0, 2):
            finish((x + 1 + d) % NX, s)
            l_x(s, d).start()
            o_x(s, d).start()
        finish(x, s)
        orecv[s, x] = osend[s, x]
        lrecv[s, x] = lsend[s, x]

    def a_x(s, i):
        ref = att.at[c, s, x]
        return copy(A_X(s, i), ref, ref, xs[i])

    def a_c(s, n):
        ref = att.at[c, s, (x + NX - n) % NX]
        return copy(A_C(s, n), ref, ref, other_c)

    def combine(s):
        for d in range(NX - 1):
            l_x(s, d).wait_recv()
            o_x(s, d).wait_recv()
        lses = [lrecv[s, i] for i in range(NX)]
        top = functools.reduce(jnp.maximum, lses)
        shares = [jnp.exp2(v - top) for v in lses]
        whole = sum(shares)
        shares = [v / whole for v in shares]
        shares.append(jnp.zeros((HD - 8 * NX, heads * some_rows), jnp.float32))
        turned = jnp.concatenate(shares, axis=0).T
        total = jnp.zeros((heads * some_rows, HD), jnp.float32)
        for i in range(NX):
            total += turned[:, 8 * i : 8 * i + 1] * orecv[s, i].astype(jnp.float32)
        total = total.astype(jnp.bfloat16)
        for g in range(heads):
            att[c, s, x, :, g * HD : (g + 1) * HD] = total[g * some_rows : (g + 1) * some_rows]
        for i in (1, 0, 2):
            a_x(s, i).start()
        a_c(s, 0).start()

    def gather(s):
        for i in (0, 2, 1):
            a_x(s, i).wait_recv()
            a_c(s, i + 1).start()

    def y_right(s, slot, peer):
        return copy(Y_R(s, slot), ysend_r.at[s, slot], yleft.at[s, slot], peer)

    def y_left(s, slot, peer):
        return copy(Y_L(s, slot), ysend_l.at[s, slot], yright.at[s, slot], peer)

    def put_right(s, slot, value, peer):
        ysend_r[s, slot] = value.astype(jnp.bfloat16)
        y_right(s, slot, peer).start()

    def put_left(s, slot, value, peer):
        ysend_l[s, slot] = value.astype(jnp.bfloat16)
        y_left(s, slot, peer).start()

    def project(s):
        for n in range(NX):
            a_c(s, n).wait_recv()
        mixed = [att[col, s].reshape(NX * some_rows, heads * HD) for col in range(NC)]

        total = jnp.zeros((NY * fw, NX * some_rows), jnp.float32)
        for col in range(NC):
            total += lax.dot_general(
                wbuf[col, c].reshape(NY * fw, heads * HD), mixed[col],
                (((1,), (1,)), ((), ())), preferred_element_type=jnp.float32,
            )
        part[s] = total.reshape(NY, fw, NX * some_rows)

        @pl.when(y == 0)
        def _():
            for dest in (3, 2, 1):
                put_right(s, dest, part[s, dest], right)

        @pl.when(y == 1)
        def _():
            put_left(s, 3, part[s, 0], left)

        @pl.when(y == 2)
        def _():
            put_right(s, 0, part[s, 3], right)

        @pl.when(y == 3)
        def _():
            for dest in (0, 1, 2):
                put_left(s, dest, part[s, dest], left)

    def sum_on(s):
        @pl.when(y == 1)
        def _():
            for dest, peer in ((3, across), (2, right)):
                y_right(s, dest, peer).wait_recv()
                put_right(s, dest, part[s, dest] + yleft[s, dest].astype(jnp.float32), peer)

        @pl.when(y == 2)
        def _():
            for dest, peer in ((0, across), (1, left)):
                y_left(s, dest, peer).wait_recv()
                put_left(s, dest, part[s, dest] + yright[s, dest].astype(jnp.float32), peer)

    def sum_up(s):
        @pl.when(y == 0)
        def _():
            y_left(s, 3, left).wait_recv()
            y_left(s, 0, across).wait_recv()
            fsum[s] = (
                part[s, 0] + yright[s, 3].astype(jnp.float32) + yright[s, 0].astype(jnp.float32)
            )

        @pl.when(y == 3)
        def _():
            y_right(s, 0, right).wait_recv()
            y_right(s, 3, across).wait_recv()
            fsum[s] = (
                part[s, 3] + yleft[s, 0].astype(jnp.float32) + yleft[s, 3].astype(jnp.float32)
            )

        for middle in (1, 2):

            @pl.when(y == middle)
            def _():
                y_right(s, middle, right).wait_recv()
                y_left(s, middle, left).wait_recv()
                fsum[s] = (
                    part[s, middle]
                    + yleft[s, middle].astype(jnp.float32)
                    + yright[s, middle].astype(jnp.float32)
                )

    def f_x(pair, d):
        place = (x + 1 + d) % NX
        return copy(F_X(pair, d), fsend.at[pair, place], frecv.at[pair, x], xs[d])

    def deliver(pair):
        first, second = fsum[2 * pair], fsum[2 * pair + 1]
        for place in range(NX):
            cols = slice(place * some_rows, (place + 1) * some_rows)
            both = jnp.concatenate([first[:, cols], second[:, cols]], axis=1)
            fsend[pair, place] = both.astype(jnp.bfloat16)
        for d in (0, 2, 1):
            f_x(pair, d).start()
        frecv[pair, x] = fsend[pair, x]

    def store(pair):
        for d in range(NX - 1):
            f_x(pair, d).wait_recv()
        tokens = slice(pair * 2 * some_rows, (pair + 1) * 2 * some_rows)
        out_ref[:, tokens] = frecv[pair].reshape(NX * fw, 2 * some_rows)

    def stage(turn, late, action, count=NS):
        pl.when((turn >= late) & (turn < late + count))(lambda: action(turn - late))

    @pl.loop(0, NS + 4)
    def _(turn):
        @pl.when(turn < NS)
        def _():
            @pl.when(z >= 4)
            def _():
                for place in range(NX):
                    tile(place, turn, ((z + NZ - 4) % NZ,), False, 1)

            send_shares(turn)

        stage(turn, 1, combine)

        @pl.when(turn == 2)
        def _():
            for direction in range(2):
                for step in range(5 - direction):
                    if step > 0 or direction == 0:
                        w_h(direction, step).wait_recv()
            for i in range(NZ // 2):
                w_c(i).start()

        stage(turn, 2, gather)

        @pl.when(turn == 2)
        def _():
            for i in range(NZ // 2):
                w_c(i).wait_recv()

        stage(turn, 2, project)

        stage(turn, 3, sum_on)

        stage(turn, 4, sum_up)

        @pl.when((turn == 5) | (turn == 7))
        def _():
            deliver((turn - 5) // 2)

    for pair in range(NS // 2):
        store(pair)

    for u in range(NU):
        kv_h(u).wait_send()
        for direction in range(2):
            for half in range(2):
                for step in range(1, 5):
                    if step < 4 or direction == half:
                        kv_z(direction, half, step, u).wait_send()
    for direction in range(2):
        for step in range(1, 5 - direction):
            w_z(direction, step).wait_send()
        for step in range(direction, 5 - direction):
            w_h(direction, step).wait_send()
    for i in range(NZ // 2):
        w_c(i).wait_send()
    for pair in range(NS // 2):
        for d in range(NX - 1):
            f_x(pair, d).wait_send()

    @pl.loop(0, NS)
    def _(s):
        for d in range(NX - 1):
            q_x(s, d).wait_send()
            l_x(s, d).wait_send()
            o_x(s, d).wait_send()
            a_x(s, d).wait_send()
        for n in range(NX):
            a_c(s, n).wait_send()

        @pl.when(y == 0)
        def _():
            for dest in (3, 2, 1):
                y_right(s, dest, right).wait_send()

        @pl.when(y == 1)
        def _():
            y_left(s, 3, left).wait_send()
            y_right(s, 3, across).wait_send()
            y_right(s, 2, right).wait_send()

        @pl.when(y == 2)
        def _():
            y_right(s, 0, right).wait_send()
            y_left(s, 0, across).wait_send()
            y_left(s, 1, left).wait_send()

        @pl.when(y == 3)
        def _():
            for dest in (0, 1, 2):
                y_left(s, dest, left).wait_send()


def body(queries, keys, values, out_weight):
    rows = queries.shape[0]
    wrows = out_weight.shape[0]
    cols = queries.shape[1]
    heads = cols // HD
    fw = NH * wrows
    some = rows // NS
    positions = lax.axis_index("ctx") * rows + jnp.arange(rows, dtype=jnp.int32)
    cosine, sines = rotation(positions)
    vmem = pl.BlockSpec(memory_space=pltpu.VMEM)
    bf16, f32 = jnp.bfloat16, jnp.float32
    turned = pl.pallas_call(
        kernel,
        out_shape=jax.ShapeDtypeStruct((NX * fw, rows), bf16),
        in_specs=[vmem] * 6,
        out_specs=vmem,
        scratch_shapes=[
            pltpu.VMEM((NX, rows, cols), bf16),
            pltpu.VMEM((NZ, NH * rows, 2 * HD), bf16),
            pltpu.VMEM((NC, 2, NZ // 2, fw, cols), bf16),
            pltpu.VMEM((NX, NS, heads * some, 2 * HD), f32),
            pltpu.VMEM((NX, NS, heads * some, HD), f32),
            pltpu.VMEM((NS, NX, heads * some, HD), bf16),
            pltpu.VMEM((NS, NX, heads * some, HD), bf16),
            pltpu.VMEM((NS, NX, 8, heads * some), f32),
            pltpu.VMEM((NS, NX, 8, heads * some), f32),
            pltpu.VMEM((NC, NS, NX, some, cols), bf16),
            pltpu.VMEM((NS, NY, fw, NX * some), f32),
            pltpu.VMEM((NS, NY, fw, NX * some), bf16),
            pltpu.VMEM((NS, NY, fw, NX * some), bf16),
            pltpu.VMEM((NS, NY, fw, NX * some), bf16),
            pltpu.VMEM((NS, NY, fw, NX * some), bf16),
            pltpu.VMEM((NS, fw, NX * some), f32),
            pltpu.VMEM((NS // 2, NX, fw, 2 * some), bf16),
            pltpu.VMEM((NS // 2, NX, fw, 2 * some), bf16),
            pltpu.SemaphoreType.DMA((COUNT,)),
            pltpu.SemaphoreType.DMA((COUNT,)),
        ],
        compiler_params=pltpu.CompilerParams(
            collective_id=0, has_side_effects=True, vmem_limit_bytes=56 * 2**20
        ),
        name="attention_layer",
    )(queries, keys, values, out_weight, cosine, sines)
    return turned.T


def solution(mesh):
    placed = (P("ctx", "tp"), P("ctx", "tp"), P("ctx", "tp"), P("ctx", "tp"))
    return jax.shard_map(
        body, mesh=mesh, in_specs=placed, out_specs=P("ctx", "tp"), check_vma=False
    )
```
